32 devices in a mesh: groups: 2 (over y), qrow: 4 (over z), db: 2 (over x), rep: 2 (over core).
Axes of the slice: x: 2, y: 2, z: 4, core: 2. Of those that a mesh axis runs over, the one named last changes fastest.
Arguments:
- queries: bfloat16 [8, 8, 8, 1024], P(('groups', 'qrow')), parts along dimension 0, may hold values from -6 to 6
- db_maps: bfloat16 [8, 256, 1024], P(('groups', 'db', 'rep')), parts along dimension 0, may hold values from -6 to 6
- round_owner: int32 [6], P('groups'), parts along dimension 0, may hold values from 0 to 3, as said below
- conv1_weight: bfloat16 [16, 3, 3, 3, 3], replicated, may hold values from -2 to 2
- conv1_bias: float32 [16], replicated, may hold values from -0.2 to 0.2
- conv2_weight: bfloat16 [16, 3, 3, 3, 3], replicated, may hold values from -0.5 to 0.5
- conv2_bias: float32 [1], replicated, may hold values from -0.3 to 0.3
Outputs:
- match_scores: float32 [3, 8, 8, 8, 256], P(None, ('groups', 'db', 'rep'), 'qrow'), parts along dimension 1
The draws below stay inside these ranges and needn't reach their ends.
There are 2 independent parts, one for each index of `groups`. The reference program is written for one: setup_inputs(seed, part) draws one part's arguments, and reference() takes and returns one part's arrays. A program takes and returns all parts, laid end to end along the dimension named above; an argument that names none is the same for every part. Nothing has to cross between parts.
Inputs may be any that keep to these rules, and one draw needn't show every extreme that they name: Round r verifies query map round_owner[r]; the rounds verify distinct maps.
All inputs are finite; a program needn't handle non-finite values.
Results may differ from the reference program's by a relative error of at most 0.0049.
Values may be sent and summed in bfloat16 or wider, within the bound.
A program may use at most 64 MiB of HBM per device.

```python
import math
import jax
import jax.numpy as jnp
from jax import lax

C = 1024
HID = 16
WQ = 8
HD = 16
WD = 16
ROUNDS = 3
HQ = 8
QUERIES = 4
MAPS = 4


def draw_round_owner(key, part):
    first_key = jax.random.fold_in(key, 11)
    second_key = jax.random.fold_in(key, 23)
    middle = 1 + jax.random.permutation(first_key, QUERIES - 2)[:ROUNDS - 2]
    values = jnp.concatenate([jnp.array([0, QUERIES - 1], jnp.int32), middle.astype(jnp.int32)])
    order = jax.random.permutation(second_key, ROUNDS)
    return jnp.take(values, order).astype(jnp.int32)


def level_of(stream_key, extent, split, least, largest):
    gain, own = 1.0, jax.random.fold_in(stream_key, 6)
    for position, shards_of in split:
        heights = jnp.exp(jax.random.uniform(jax.random.fold_in(own, position), (shards_of,), jnp.float32, least / len(split), largest / len(split)))
        gain = gain * jnp.repeat(heights, extent[position] // shards_of).reshape([-1 if axis == position else 1 for axis in range(len(extent))])
    return gain


def bell_draw(stream_key, dims, deviation, bound, shards=(), dtype=jnp.bfloat16):
    values = jax.random.normal(stream_key, dims, jnp.float32) * deviation
    if len(shards) > 0:
        values = level_of(stream_key, dims, shards, -0.22, 0.18) * values
    return jnp.clip(values, min=-bound, max=bound).astype(dtype)


def setup_inputs(seed: int = 0, part: int = 0) -> dict:
    key_of = jax.random.split(jax.random.key(seed), 8)
    own_keys = jax.random.split(jax.random.fold_in(key_of[7], part), 8)
    return {
        "queries": bell_draw(own_keys[0], (QUERIES, HQ, WQ, C), 1.0, 6.0, ((0, 4),)),
        "db_maps": bell_draw(own_keys[1], (MAPS, HD * WD, C), 1.0, 6.0, ((0, 4),)),
        "round_owner": draw_round_owner(jax.random.fold_in(jax.random.fold_in(key_of[7], part), 71), part),
        "conv1_weight": bell_draw(key_of[3], (HID, 3, 3, 3, 3), 9 ** -0.5, 2.0),
        "conv1_bias": jnp.clip(jax.random.uniform(key_of[4], (HID,), jnp.float32, -0.2, 0.2), -0.2, 0.2),
        "conv2_weight": bell_draw(key_of[5], (HID, 3, 3, 3, 3), 144 ** -0.5, 0.5),
        "conv2_bias": jnp.clip(jax.random.uniform(key_of[6], (1,), jnp.float32, -0.3, 0.3), -0.3, 0.3),
    }


epsilon = 1e-05

def db_tap(flattened, shift_k, shift_l):
    leading = flattened.shape[:-1]
    lattice = flattened.reshape(leading + (HD, WD))
    padded = jnp.pad(lattice, [(0, 0)] * len(leading) + [(1, 1), (1, 1)])
    return padded[..., shift_k:shift_k + HD, shift_l:shift_l + WD].reshape(flattened.shape)

def first_conv(scores_in, first_weight, first_bias):
    count = scores_in.shape[0] - 2
    width = scores_in.shape[1]
    widened = jnp.pad(scores_in, ((0, 0), (1, 1), (0, 0)))
    shifted = jnp.stack([db_tap(widened, shift_k, shift_l) for shift_k in range(3) for shift_l in range(3)])
    stacked = jnp.stack([shifted[:, shift_i:shift_i + count, shift_j:shift_j + width] for shift_i in range(3) for shift_j in range(3)])
    channels = first_weight.shape[0]
    summed = jnp.dot(first_weight.reshape(channels, 81), stacked.reshape(81, -1), preferred_element_type=jnp.float32)
    summed = summed + first_bias[:, None]
    return jnp.maximum(summed, 0.0).reshape(channels, count, width, scores_in.shape[2])

def second_conv(hidden_in, second_weight, second_bias):
    channels = hidden_in.shape[0]
    count = hidden_in.shape[1] - 2
    width = hidden_in.shape[2]
    positions = hidden_in.shape[3]
    widened = jnp.pad(hidden_in, ((0, 0), (0, 0), (1, 1), (0, 0)))
    arranged = second_weight.reshape(channels, 3, 3, 9)
    mixture = jnp.zeros((9, count * width * positions), jnp.float32)
    for shift_i in range(3):
        selected = jnp.stack([widened[:, shift_i:shift_i + count, shift_j:shift_j + width] for shift_j in range(3)])
        taps_now = jnp.transpose(arranged[:, shift_i], (2, 1, 0)).reshape(9, 3 * channels)
        mixture = mixture + jnp.dot(taps_now, selected.reshape(3 * channels, -1), preferred_element_type=jnp.float32)
    mixture = mixture.reshape(9, count, width, positions)
    total = jnp.zeros((count, width, positions), jnp.float32)
    for shift_k in range(3):
        for shift_l in range(3):
            total = total + db_tap(mixture[shift_k * 3 + shift_l], shift_k, shift_l)
    return jnp.maximum(total + second_bias[0], 0.0)

def reference(queries, db_maps, round_owner, conv1_weight, conv1_bias, conv2_weight, conv2_bias):
    factor = 1.0 / math.sqrt(C)
    outcomes = []
    for round_index in range(ROUNDS):
        query_map = lax.dynamic_index_in_dim(queries, round_owner[round_index], 0, keepdims=False)
        flattened = query_map.reshape(HQ * WQ, C)

        def verify(db_map):
            corr = jnp.dot(flattened, db_map.T, preferred_element_type=jnp.float32) * factor
            scores = jnp.maximum(corr, 0.0)
            col_max = lax.optimization_barrier(jnp.max(scores, axis=0))
            row_max = lax.optimization_barrier(jnp.max(scores, axis=1))
            mutual = scores * (scores / (col_max[None, :] + epsilon)) * (scores / (row_max[:, None] + epsilon))
            mutual = mutual.astype(jnp.bfloat16).reshape(HQ, WQ, HD * WD)
            padded = jnp.pad(mutual, ((1, 1), (0, 0), (0, 0)))
            hidden = first_conv(padded, conv1_weight, conv1_bias).astype(jnp.bfloat16)
            hidden = jnp.pad(hidden, ((0, 0), (1, 1), (0, 0), (0, 0)))
            return second_conv(hidden, conv2_weight, conv2_bias)
        outcomes.append(lax.map(verify, db_maps))
    return jnp.stack(outcomes)
```

```python
import functools
import math

import jax
import jax.numpy as jnp
import numpy as np
from jax import lax
from jax.experimental import pallas as pl
from jax.experimental.pallas import tpu as pltpu
from jax.sharding import PartitionSpec as P

epsilon = 1e-05
TAPS = 9
SLOTS = 10
LANE_STEP = 256


def spread_tables(width, channels):
    block = SLOTS * width
    pick1 = np.zeros((81, 3 * LANE_STEP), np.float32)
    for b in range(3):
        for a in range(3):
            for cd in range(TAPS):
                start = b * LANE_STEP + a * block + cd * width
                pick1[a * 27 + b * 9 + cd, start : start + width] = 1
    lane = np.arange(LANE_STEP)
    row = np.arange(channels * width)
    band1 = (lane % width)[None, :] - (row % width)[:, None] + 1
    pick2 = np.zeros((9, TAPS, width, 81), np.float32)
    for a in range(3):
        for b in range(3):
            for cd in range(TAPS):
                pick2[a * 3 + b, cd, :, a * 27 + b * 9 + cd] = 1
    repeat2 = np.repeat(np.eye(channels, dtype=np.float32), width, axis=1)
    row = np.arange(TAPS * width)
    lane = np.arange(channels * width)
    band2 = (lane % width)[None, :] - (row % width)[:, None] + 1
    return (
        jnp.asarray(pick1, jnp.bfloat16),
        jnp.asarray(band1, jnp.int32),
        jnp.asarray(pick2.reshape(81 * width, 81), jnp.bfloat16),
        jnp.asarray(repeat2, jnp.bfloat16),
        jnp.asarray(band2, jnp.int32),
    )


def banded(band, parts):
    zero = jnp.zeros_like(parts[0])
    return jnp.where(
        band == 0, parts[0], jnp.where(band == 1, parts[1], jnp.where(band == 2, parts[2], zero))
    )


def kernel(
    count,
    width,
    side,
    owner_ref,
    bias1_ref,
    bias2_ref,
    query_ref,
    map_ref,
    weight1_ref,
    weight2_ref,
    pick1_ref,
    band1_ref,
    pick2_ref,
    repeat2_ref,
    band2_ref,
    out_ref,
    shifted,
    result,
    received,
    send_sem,
    recv_sem,
):
    me = lax.axis_index("qrow")
    barrier = pltpu.get_barrier_semaphore()
    for step in range(1, count):
        pl.semaphore_signal(
            barrier,
            inc=1,
            device_id={"qrow": lax.rem(me + step, count)},
            device_id_type=pl.DeviceIdType.MESH,
        )

    positions = map_ref.shape[0]
    rows = query_ref.shape[0] // width
    channels = weight1_ref.shape[0]
    block = SLOTS * width

    chosen = jnp.dot(weight1_ref[...], pick1_ref[...], preferred_element_type=jnp.float32)
    parts = [
        jnp.broadcast_to(
            chosen[:, b * LANE_STEP : (b + 1) * LANE_STEP][:, None, :],
            (channels, width, LANE_STEP),
        ).reshape(channels * width, LANE_STEP)
        for b in range(3)
    ]
    matrix1 = banded(band1_ref[...], parts).astype(jnp.bfloat16)[:, : 3 * block]

    wide = lax.dot_general(
        weight2_ref[...],
        repeat2_ref[...],
        (((0,), (0,)), ((), ())),
        preferred_element_type=jnp.float32,
    ).astype(jnp.bfloat16)
    tall = jnp.dot(pick2_ref[...], wide, preferred_element_type=jnp.float32)
    band2 = band2_ref[...]
    size = TAPS * width
    matrix2 = jnp.concatenate(
        [
            banded(band2, [tall[(a * 3 + b) * size : (a * 3 + b + 1) * size] for b in range(3)])
            for a in range(3)
        ],
        axis=0,
    ).astype(jnp.bfloat16)

    corr = lax.dot_general(
        query_ref[...],
        map_ref[...],
        (((1,), (1,)), ((), ())),
        preferred_element_type=jnp.float32,
    ) * (1.0 / math.sqrt(query_ref.shape[1]))
    scores = jnp.maximum(corr, 0.0)
    col_scale = 1.0 / (jnp.max(scores, axis=0, keepdims=True) + epsilon)
    row_scale = 1.0 / (jnp.max(scores, axis=1, keepdims=True) + epsilon)
    mutual = scores * (scores * col_scale) * (scores * row_scale)

    lane = lax.broadcasted_iota(jnp.int32, (1, positions), 1)
    column = lane & (side - 1)

    def inner(value, d):
        if d == 1:
            return value
        moved = pltpu.roll(value, (1 - d) % positions, 1)
        return jnp.where(column == (0 if d == 0 else side - 1), 0.0, moved)

    def outer(value, c):
        if c == 1:
            return value
        moved = pltpu.roll(value, ((1 - c) * side) % positions, 1)
        edge = lane < side if c == 0 else lane >= positions - side
        return jnp.where(edge, 0.0, moved)

    along = [inner(mutual, d) for d in range(3)]
    taps = [outer(along[d], c) for c in range(3) for d in range(3)]
    blank = jnp.zeros((block, positions), jnp.bfloat16)
    shifted[pl.ds(0, block), :] = blank
    shifted[pl.ds((rows + 1) * block, block), :] = blank
    gap = jnp.zeros((width, positions), jnp.float32)
    for i in range(rows):
        shifted[pl.ds((i + 1) * block, block), :] = jnp.concatenate(
            [tap[i * width : (i + 1) * width] for tap in taps] + [gap], axis=0
        ).astype(jnp.bfloat16)

    bias1 = jnp.concatenate(
        [jnp.full((width, positions), bias1_ref[o], jnp.float32) for o in range(channels)], axis=0
    )
    mixed = []
    for i in range(rows):
        hidden = jnp.dot(
            matrix1, shifted[pl.ds(i * block, 3 * block), :], preferred_element_type=jnp.float32
        )
        hidden = jnp.maximum(hidden + bias1, 0.0).astype(jnp.bfloat16)
        mixed.append(jnp.dot(matrix2, hidden, preferred_element_type=jnp.float32))

    each = rows // count
    for target in range(count):
        totals = []
        for i in range(target * each, (target + 1) * each):
            summed = mixed[i][size : 2 * size]
            if i > 0:
                summed = summed + mixed[i - 1][:size]
            if i < rows - 1:
                summed = summed + mixed[i + 1][2 * size :]
            total = None
            for c in range(3):
                row = None
                for d in range(3):
                    tap = (c * 3 + d) * width
                    term = inner(summed[tap : tap + width], d)
                    row = term if row is None else row + term
                row = outer(row, c)
                total = row if total is None else total + row
            totals.append(jnp.maximum(total + bias2_ref[0], 0.0))
        result[target] = jnp.concatenate(totals, axis=0)

    pl.semaphore_wait(barrier, count - 1)

    def transfer(source, target):
        return pltpu.make_async_remote_copy(
            src_ref=result.at[target],
            dst_ref=received.at[source],
            send_sem=send_sem.at[target],
            recv_sem=recv_sem.at[source],
            device_id={"qrow": target},
            device_id_type=pl.DeviceIdType.MESH,
        )

    for step in range(1, count):
        transfer(me, lax.rem(me + step, count)).start()
    received[me] = result[me]
    for step in range(1, count):
        transfer(lax.rem(me + step, count), me).wait_recv()
    for r in range(out_ref.shape[0]):
        out_ref[r] = received[owner_ref[r]]
    for step in range(1, count):
        transfer(me, lax.rem(me + step, count)).wait_send()


def on_device(count, queries, db_maps, round_owner, conv1_weight, conv1_bias, conv2_weight, conv2_bias):
    maps, rows, width, depth = queries.shape
    positions = db_maps.shape[1]
    channels = conv1_weight.shape[0]
    side = math.isqrt(positions)
    each = rows // count
    tables = spread_tables(width, channels)
    scalars = pl.BlockSpec(memory_space=pltpu.SMEM)
    vectors = pl.BlockSpec(memory_space=pltpu.VMEM)
    block = SLOTS * width
    rounds = round_owner.shape[0]
    result = pl.pallas_call(
        functools.partial(kernel, count, width, side),
        out_shape=jax.ShapeDtypeStruct((rounds, each * width, positions), jnp.float32),
        in_specs=[scalars] * 3 + [vectors] * 9,
        out_specs=vectors,
        scratch_shapes=[
            pltpu.VMEM(((rows + 2) * block, positions), jnp.bfloat16),
            pltpu.VMEM((count, each * width, positions), jnp.float32),
            pltpu.VMEM((count, each * width, positions), jnp.float32),
            pltpu.SemaphoreType.DMA((count,)),
            pltpu.SemaphoreType.DMA((count,)),
        ],
        compiler_params=pltpu.CompilerParams(
            collective_id=0, has_side_effects=True, vmem_limit_bytes=48 * 1024 * 1024
        ),
        name="verify",
    )(
        round_owner,
        conv1_bias,
        conv2_bias,
        queries.reshape(maps * rows * width, depth),
        db_maps.reshape(positions, depth),
        conv1_weight.reshape(channels, 81),
        conv2_weight.reshape(channels, 81),
        *tables,
    )
    return result.reshape(rounds, 1, each, width, positions)


def solution(mesh):
    placed = (
        P(("groups", "qrow"), None, None, None),
        P(("groups", "db", "rep"), None, None),
        P("groups"),
        P(),
        P(),
        P(),
        P(),
    )
    return jax.shard_map(
        functools.partial(on_device, mesh.shape["qrow"]),
        mesh=mesh,
        in_specs=placed,
        out_specs=P(None, ("groups", "db", "rep"), "qrow", None, None),
        check_vma=False,
    )
```

```python
import functools
import math

import jax
import jax.numpy as jnp
from jax import lax
from jax.experimental import pallas as pl
from jax.experimental.pallas import tpu as pltpu
from jax.sharding import PartitionSpec as P

epsilon = 1e-05
TAPS = 9
SLOTS = 10
LANE_STEP = 256
STRIDE = 32


def tap_row(a, b, c, d):
    return d * STRIDE + (a * 3 + b) * 3 + c


def tap_matrix(weight_ref, spread):
    spread[...] = jnp.zeros_like(spread)
    groups, inner, channels = weight_ref.shape
    values = weight_ref[...].astype(jnp.float32)
    for d in range(inner):
        spread[pl.ds(d * STRIDE, groups), pl.ds(0, channels)] = values[:, d, :]
    return spread[...][:, :channels].astype(jnp.bfloat16)


def banded(masks, parts):
    value = jnp.zeros(masks[0].shape, jnp.float32)
    for mask, part in zip(masks, parts):
        value = jnp.where(mask, jnp.broadcast_to(part, mask.shape), value)
    return value


def first_matrix(taps, width, chosen_ref):
    rows, channels = taps.shape
    block = SLOTS * width
    lane = lax.broadcasted_iota(jnp.int32, (1, LANE_STEP), 1)
    a = sum((lane >= k * block).astype(jnp.int32) for k in (1, 2))
    offset = lane - a * block
    tap = sum((offset >= k * width).astype(jnp.int32) for k in range(1, SLOTS))
    c = (tap >= 3).astype(jnp.int32) + (tap >= 6).astype(jnp.int32)
    d = tap - 3 * c
    valid = (tap < TAPS) & (lane < 3 * block)
    base = jnp.where(valid, d * STRIDE + a * 9 + c, -rows)
    row = lax.broadcasted_iota(jnp.int32, (rows, LANE_STEP), 0)
    for b in range(3):
        pick = jnp.where(row == base + 3 * b, 1.0, 0.0).astype(jnp.bfloat16)
        chosen_ref[b] = lax.dot_general(
            taps, pick, (((0,), (0,)), ((), ())), preferred_element_type=jnp.float32
        )
    band = offset - tap * width - lax.broadcasted_iota(jnp.int32, (width, LANE_STEP), 0) + 1
    masks = [band == b for b in range(3)]
    return jnp.concatenate(
        [
            banded(masks, [chosen_ref[b, pl.ds(o, 1), :] for b in range(3)])
            for o in range(channels)
        ],
        axis=0,
    ).astype(jnp.bfloat16)[:, : 3 * block]


def second_matrix(taps, width, wide_ref):
    channels = taps.shape[1]
    lanes = channels * width
    lane = lax.broadcasted_iota(jnp.int32, (channels, lanes), 1)
    start = lax.broadcasted_iota(jnp.int32, (channels, lanes), 0) * width
    repeat = jnp.where((lane >= start) & (lane < start + width), 1.0, 0.0).astype(jnp.bfloat16)
    wide_ref[...] = jnp.dot(taps, repeat, preferred_element_type=jnp.float32)
    channel = sum(
        (lax.broadcasted_iota(jnp.int32, (1, lanes), 1) >= k * width).astype(jnp.int32)
        for k in range(1, channels)
    )
    column = lax.broadcasted_iota(jnp.int32, (1, lanes), 1) - channel * width
    band = column - lax.broadcasted_iota(jnp.int32, (width, lanes), 0) + 1
    masks = [band == b for b in range(3)]
    return jnp.concatenate(
        [
            banded(masks, [wide_ref[pl.ds(tap_row(a, b, c, d), 1), :] for b in range(3)])
            for a in range(3)
            for c in range(3)
            for d in range(3)
        ],
        axis=0,
    ).astype(jnp.bfloat16)


def kernel(
    count,
    width,
    side,
    owner_hbm,
    bias1_hbm,
    bias2_hbm,
    query_hbm,
    map_hbm,
    weight1_hbm,
    weight2_hbm,
    out_ref,
    owner_ref,
    bias1_ref,
    bias2_ref,
    query_ref,
    map_ref,
    weight1_ref,
    weight2_ref,
    spread1,
    spread2,
    chosen,
    wide,
    shifted,
    result,
    received,
    load_sem,
    send_sem,
    recv_sem,
):
    loads = [
        pltpu.make_async_copy(source, target, load_sem.at[index])
        for index, (source, target) in enumerate(
            (
                (weight1_hbm, weight1_ref),
                (weight2_hbm, weight2_ref),
                (map_hbm, map_ref),
                (query_hbm, query_ref),
                (bias1_hbm, bias1_ref),
                (bias2_hbm, bias2_ref),
                (owner_hbm, owner_ref),
            )
        )
    ]
    for load in loads:
        load.start()
    me = lax.axis_index("qrow")
    barrier = pltpu.get_barrier_semaphore()
    for step in range(1, count):
        pl.semaphore_signal(
            barrier,
            inc=1,
            device_id={"qrow": lax.rem(me + step, count)},
            device_id_type=pl.DeviceIdType.MESH,
        )

    positions = map_ref.shape[0]
    rows = query_ref.shape[0] // width
    channels = weight1_ref.shape[2]
    block = SLOTS * width
    size = TAPS * width

    loads[0].wait()
    loads[1].wait()
    matrix1 = first_matrix(tap_matrix(weight1_ref, spread1), width, chosen)
    matrix2 = second_matrix(tap_matrix(weight2_ref, spread2), width, wide)
    for load in loads[2:]:
        load.wait()

    corr = lax.dot_general(
        query_ref[...],
        map_ref[...],
        (((1,), (1,)), ((), ())),
        preferred_element_type=jnp.float32,
    ) * (1.0 / math.sqrt(query_ref.shape[1]))
    scores = jnp.maximum(corr, 0.0)
    col_scale = 1.0 / (jnp.max(scores, axis=0, keepdims=True) + epsilon)
    row_scale = 1.0 / (jnp.max(scores, axis=1, keepdims=True) + epsilon)
    mutual = scores * (scores * col_scale) * (scores * row_scale)

    lane = lax.broadcasted_iota(jnp.int32, (1, positions), 1)
    column = lane & (side - 1)

    def inner(value, d):
        if d == 1:
            return value
        moved = pltpu.roll(value, (1 - d) % positions, 1)
        return jnp.where(column == (0 if d == 0 else side - 1), 0.0, moved)

    def outer(value, c):
        if c == 1:
            return value
        moved = pltpu.roll(value, ((1 - c) * side) % positions, 1)
        edge = lane < side if c == 0 else lane >= positions - side
        return jnp.where(edge, 0.0, moved)

    along = [inner(mutual, d) for d in range(3)]
    taps = [outer(along[d], c) for c in range(3) for d in range(3)]
    blank = jnp.zeros((block, positions), jnp.bfloat16)
    shifted[pl.ds(0, block), :] = blank
    shifted[pl.ds((rows + 1) * block, block), :] = blank
    gap = jnp.zeros((width, positions), jnp.float32)
    for i in range(rows):
        shifted[pl.ds((i + 1) * block, block), :] = jnp.concatenate(
            [tap[i * width : (i + 1) * width] for tap in taps] + [gap], axis=0
        ).astype(jnp.bfloat16)

    bias1 = jnp.concatenate(
        [jnp.full((width, positions), bias1_ref[o], jnp.float32) for o in range(channels)], axis=0
    )
    mixed = []
    for i in range(rows):
        hidden = jnp.dot(
            matrix1, shifted[pl.ds(i * block, 3 * block), :], preferred_element_type=jnp.float32
        )
        hidden = jnp.maximum(hidden + bias1, 0.0).astype(jnp.bfloat16)
        mixed.append(jnp.dot(matrix2, hidden, preferred_element_type=jnp.float32))

    each = rows // count
    for target in range(count):
        totals = []
        for i in range(target * each, (target + 1) * each):
            summed = mixed[i][size : 2 * size]
            if i > 0:
                summed = summed + mixed[i - 1][:size]
            if i < rows - 1:
                summed = summed + mixed[i + 1][2 * size :]
            total = None
            for c in range(3):
                row = None
                for d in range(3):
                    tap = (c * 3 + d) * width
                    term = inner(summed[tap : tap + width], d)
                    row = term if row is None else row + term
                row = outer(row, c)
                total = row if total is None else total + row
            totals.append(jnp.maximum(total + bias2_ref[0], 0.0))
        result[target] = jnp.concatenate(totals, axis=0)

    pl.semaphore_wait(barrier, count - 1)

    def transfer(source, target):
        return pltpu.make_async_remote_copy(
            src_ref=result.at[target],
            dst_ref=received.at[source],
            send_sem=send_sem.at[target],
            recv_sem=recv_sem.at[source],
            device_id={"qrow": target},
            device_id_type=pl.DeviceIdType.MESH,
        )

    for step in range(1, count):
        transfer(me, lax.rem(me + step, count)).start()
    received[me] = result[me]
    for step in range(1, count):
        transfer(lax.rem(me + step, count), me).wait_recv()
    for r in range(out_ref.shape[0]):
        out_ref[r] = received[owner_ref[r]]
    for step in range(1, count):
        transfer(me, lax.rem(me + step, count)).wait_send()


def on_device(count, queries, db_maps, round_owner, conv1_weight, conv1_bias, conv2_weight, conv2_bias):
    maps, rows, width, depth = queries.shape
    positions = db_maps.shape[1]
    channels = conv1_weight.shape[0]
    side = math.isqrt(positions)
    each = rows // count
    block = SLOTS * width
    rounds = round_owner.shape[0]

    def taps_first(weight):
        return jnp.transpose(weight, (1, 2, 3, 4, 0)).reshape(27, 3, channels)

    result = pl.pallas_call(
        functools.partial(kernel, count, width, side),
        out_shape=jax.ShapeDtypeStruct((rounds, each * width, positions), jnp.float32),
        in_specs=[pl.BlockSpec(memory_space=pltpu.HBM)] * 7,
        out_specs=pl.BlockSpec(memory_space=pltpu.VMEM),
        scratch_shapes=[
            pltpu.SMEM((rounds,), jnp.int32),
            pltpu.SMEM((channels,), jnp.float32),
            pltpu.SMEM((1,), jnp.float32),
            pltpu.VMEM((rows * width, depth), jnp.bfloat16),
            pltpu.VMEM((positions, depth), jnp.bfloat16),
            pltpu.VMEM((27, 3, channels), jnp.bfloat16),
            pltpu.VMEM((27, 3, channels), jnp.bfloat16),
            pltpu.VMEM((3 * STRIDE, 128), jnp.float32),
            pltpu.VMEM((3 * STRIDE, 128), jnp.float32),
            pltpu.VMEM((3, channels, LANE_STEP), jnp.float32),
            pltpu.VMEM((3 * STRIDE, channels * width), jnp.float32),
            pltpu.VMEM(((rows + 2) * block, positions), jnp.bfloat16),
            pltpu.VMEM((count, each * width, positions), jnp.float32),
            pltpu.VMEM((count, each * width, positions), jnp.float32),
            pltpu.SemaphoreType.DMA((7,)),
            pltpu.SemaphoreType.DMA((count,)),
            pltpu.SemaphoreType.DMA((count,)),
        ],
        compiler_params=pltpu.CompilerParams(
            collective_id=0, has_side_effects=True, vmem_limit_bytes=60 * 1024 * 1024
        ),
        name="verify",
    )(
        round_owner,
        conv1_bias,
        conv2_bias,
        queries.reshape(maps * rows * width, depth),
        db_maps.reshape(positions, depth),
        taps_first(conv1_weight),
        taps_first(conv2_weight),
    )
    return result.reshape(rounds, 1, each, width, positions)


def solution(mesh):
    placed = (
        P(("groups", "qrow"), None, None, None),
        P(("groups", "db", "rep"), None, None),
        P("groups"),
        P(),
        P(),
        P(),
        P(),
    )
    return jax.shard_map(
        functools.partial(on_device, mesh.shape["qrow"]),
        mesh=mesh,
        in_specs=placed,
        out_specs=P(None, ("groups", "db", "rep"), "qrow", None, None),
        check_vma=False,
    )
```

```python
import functools
import math

import jax
import jax.numpy as jnp
from jax import lax
from jax.experimental import pallas as pl
from jax.experimental.pallas import tpu as pltpu
from jax.sharding import PartitionSpec as P

epsilon = 1e-05
TAPS = 9
SLOTS = 10
LANE_STEP = 256
STRIDE = 8
GROUPS = 28


def tap_row(a, b, c, d):
    return ((a * 3 + b) * 3 + c) * STRIDE + d


def tap_matrix(weight_ref, spread):
    groups, inner, channels = weight_ref.shape
    spread[pl.ds(0, groups), pl.ds(0, inner), :] = weight_ref[...].astype(jnp.float32)
    return spread[...].reshape(GROUPS * STRIDE, channels).astype(jnp.bfloat16)


def banded(masks, parts):
    value = jnp.zeros(masks[0].shape, jnp.float32)
    for mask, part in zip(masks, parts):
        value = jnp.where(mask, jnp.broadcast_to(part, mask.shape), value)
    return value


def fill_picks(width, pick_ref):
    rows = GROUPS * STRIDE
    block = SLOTS * width
    lane = lax.broadcasted_iota(jnp.int32, (1, LANE_STEP), 1)
    a = sum((lane >= k * block).astype(jnp.int32) for k in (1, 2))
    offset = lane - a * block
    tap = sum((offset >= k * width).astype(jnp.int32) for k in range(1, SLOTS))
    c = (tap >= 3).astype(jnp.int32) + (tap >= 6).astype(jnp.int32)
    d = tap - 3 * c
    valid = (tap < TAPS) & (lane < 3 * block)
    base = jnp.where(valid, tap_row(a, 0, c, d), -2 * rows)
    row = lax.broadcasted_iota(jnp.int32, (rows, LANE_STEP), 0)
    for b in range(3):
        pick_ref[b] = jnp.where(row == base + tap_row(0, b, 0, 0), 1.0, 0.0).astype(jnp.bfloat16)
    return offset - tap * width - lax.broadcasted_iota(jnp.int32, (width, LANE_STEP), 0) + 1


def first_matrix(taps, width, pick_ref, band, chosen_ref):
    for b in range(3):
        chosen_ref[b] = lax.dot_general(
            taps, pick_ref[b], (((0,), (0,)), ((), ())), preferred_element_type=jnp.float32
        )
    masks = [band == b for b in range(3)]
    return jnp.concatenate(
        [
            banded(masks, [chosen_ref[b, pl.ds(o, 1), :] for b in range(3)])
            for o in range(taps.shape[1])
        ],
        axis=0,
    ).astype(jnp.bfloat16)[:, : 3 * SLOTS * width]


def second_matrix(taps, width, wide_ref):
    channels = taps.shape[1]
    lanes = channels * width
    lane = lax.broadcasted_iota(jnp.int32, (channels, lanes), 1)
    start = lax.broadcasted_iota(jnp.int32, (channels, lanes), 0) * width
    repeat = jnp.where((lane >= start) & (lane < start + width), 1.0, 0.0).astype(jnp.bfloat16)
    wide_ref[...] = jnp.dot(taps, repeat, preferred_element_type=jnp.float32)
    channel = sum(
        (lax.broadcasted_iota(jnp.int32, (1, lanes), 1) >= k * width).astype(jnp.int32)
        for k in range(1, channels)
    )
    column = lax.broadcasted_iota(jnp.int32, (1, lanes), 1) - channel * width
    band = column - lax.broadcasted_iota(jnp.int32, (width, lanes), 0) + 1
    masks = [band == b for b in range(3)]
    return jnp.concatenate(
        [
            banded(masks, [wide_ref[pl.ds(tap_row(a, b, c, d), 1), :] for b in range(3)])
            for a in range(3)
            for c in range(3)
            for d in range(3)
        ],
        axis=0,
    ).astype(jnp.bfloat16)


def kernel(
    count,
    width,
    side,
    owner_hbm,
    bias1_hbm,
    bias2_hbm,
    query_hbm,
    map_hbm,
    weight1_hbm,
    weight2_hbm,
    out_ref,
    owner_ref,
    bias1_ref,
    bias2_ref,
    query_ref,
    map_ref,
    weight1_ref,
    weight2_ref,
    spread1,
    spread2,
    pick,
    chosen,
    wide,
    shifted,
    result,
    received,
    load_sem,
    send_sem,
    recv_sem,
):
    loads = [
        pltpu.make_async_copy(source, target, load_sem.at[index])
        for index, (source, target) in enumerate(
            (
                (weight1_hbm, weight1_ref),
                (weight2_hbm, weight2_ref),
                (map_hbm, map_ref),
                (query_hbm, query_ref),
                (bias1_hbm, bias1_ref),
                (bias2_hbm, bias2_ref),
                (owner_hbm, owner_ref),
            )
        )
    ]
    for load in loads:
        load.start()
    me = lax.axis_index("qrow")
    barrier = pltpu.get_barrier_semaphore()
    for step in range(1, count):
        pl.semaphore_signal(
            barrier,
            inc=1,
            device_id={"qrow": lax.rem(me + step, count)},
            device_id_type=pl.DeviceIdType.MESH,
        )

    positions = map_ref.shape[0]
    rows = query_ref.shape[0] // width
    channels = weight1_ref.shape[2]
    block = SLOTS * width
    size = TAPS * width

    band = fill_picks(width, pick)
    for spread in (spread1, spread2):
        spread[...] = jnp.zeros_like(spread)
    blank = jnp.zeros((block, positions), jnp.bfloat16)
    shifted[pl.ds(0, block), :] = blank
    shifted[pl.ds((rows + 1) * block, block), :] = blank
    for load in loads:
        load.wait()

    matrix1 = first_matrix(tap_matrix(weight1_ref, spread1), width, pick, band, chosen)
    matrix2 = second_matrix(tap_matrix(weight2_ref, spread2), width, wide)

    corr = lax.dot_general(
        query_ref[...],
        map_ref[...],
        (((1,), (1,)), ((), ())),
        preferred_element_type=jnp.float32,
    ) * (1.0 / math.sqrt(query_ref.shape[1]))
    scores = jnp.maximum(corr, 0.0)
    col_scale = 1.0 / (jnp.max(scores, axis=0, keepdims=True) + epsilon)
    row_scale = 1.0 / (jnp.max(scores, axis=1, keepdims=True) + epsilon)
    mutual = scores * (scores * col_scale) * (scores * row_scale)

    lane = lax.broadcasted_iota(jnp.int32, (1, positions), 1)
    column = lane & (side - 1)

    def inner(value, d):
        if d == 1:
            return value
        moved = pltpu.roll(value, (1 - d) % positions, 1)
        return jnp.where(column == (0 if d == 0 else side - 1), 0.0, moved)

    def outer(value, c):
        if c == 1:
            return value
        moved = pltpu.roll(value, ((1 - c) * side) % positions, 1)
        edge = lane < side if c == 0 else lane >= positions - side
        return jnp.where(edge, 0.0, moved)

    along = [inner(mutual, d) for d in range(3)]
    taps = [outer(along[d], c) for c in range(3) for d in range(3)]
    gap = jnp.zeros((width, positions), jnp.float32)
    for i in range(rows):
        shifted[pl.ds((i + 1) * block, block), :] = jnp.concatenate(
            [tap[i * width : (i + 1) * width] for tap in taps] + [gap], axis=0
        ).astype(jnp.bfloat16)

    bias1 = jnp.concatenate(
        [jnp.full((width, positions), bias1_ref[o], jnp.float32) for o in range(channels)], axis=0
    )
    mixed = []
    for i in range(rows):
        hidden = jnp.dot(
            matrix1, shifted[pl.ds(i * block, 3 * block), :], preferred_element_type=jnp.float32
        )
        hidden = jnp.maximum(hidden + bias1, 0.0).astype(jnp.bfloat16)
        mixed.append(jnp.dot(matrix2, hidden, preferred_element_type=jnp.float32))

    each = rows // count
    for target in range(count):
        totals = []
        for i in range(target * each, (target + 1) * each):
            summed = mixed[i][size : 2 * size]
            if i > 0:
                summed = summed + mixed[i - 1][:size]
            if i < rows - 1:
                summed = summed + mixed[i + 1][2 * size :]
            total = None
            for c in range(3):
                row = None
                for d in range(3):
                    tap = (c * 3 + d) * width
                    term = inner(summed[tap : tap + width], d)
                    row = term if row is None else row + term
                row = outer(row, c)
                total = row if total is None else total + row
            totals.append(jnp.maximum(total + bias2_ref[0], 0.0))
        result[target] = jnp.concatenate(totals, axis=0).astype(jnp.bfloat16)

    pl.semaphore_wait(barrier, count - 1)

    def transfer(source, target):
        return pltpu.make_async_remote_copy(
            src_ref=result.at[target],
            dst_ref=received.at[source],
            send_sem=send_sem.at[target],
            recv_sem=recv_sem.at[source],
            device_id={"qrow": target},
            device_id_type=pl.DeviceIdType.MESH,
        )

    for step in range(1, count):
        transfer(me, lax.rem(me + step, count)).start()
    received[me] = result[me]
    for step in range(1, count):
        transfer(lax.rem(me + step, count), me).wait_recv()
    for r in range(out_ref.shape[0]):
        out_ref[r] = received[owner_ref[r]].astype(jnp.float32)
    for step in range(1, count):
        transfer(me, lax.rem(me + step, count)).wait_send()


def on_device(count, queries, db_maps, round_owner, conv1_weight, conv1_bias, conv2_weight, conv2_bias):
    maps, rows, width, depth = queries.shape
    positions = db_maps.shape[1]
    channels = conv1_weight.shape[0]
    side = math.isqrt(positions)
    each = rows // count
    block = SLOTS * width
    rounds = round_owner.shape[0]

    def taps_first(weight):
        return jnp.transpose(weight, (1, 2, 3, 4, 0)).reshape(27, 3, channels)

    result = pl.pallas_call(
        functools.partial(kernel, count, width, side),
        out_shape=jax.ShapeDtypeStruct((rounds, each * width, positions), jnp.float32),
        in_specs=[pl.BlockSpec(memory_space=pltpu.HBM)] * 7,
        out_specs=pl.BlockSpec(memory_space=pltpu.VMEM),
        scratch_shapes=[
            pltpu.SMEM((rounds,), jnp.int32),
            pltpu.SMEM((channels,), jnp.float32),
            pltpu.SMEM((1,), jnp.float32),
            pltpu.VMEM((rows * width, depth), jnp.bfloat16),
            pltpu.VMEM((positions, depth), jnp.bfloat16),
            pltpu.VMEM((27, 3, channels), jnp.bfloat16),
            pltpu.VMEM((27, 3, channels), jnp.bfloat16),
            pltpu.VMEM((GROUPS, STRIDE, channels), jnp.float32),
            pltpu.VMEM((GROUPS, STRIDE, channels), jnp.float32),
            pltpu.VMEM((3, GROUPS * STRIDE, LANE_STEP), jnp.bfloat16),
            pltpu.VMEM((3, channels, LANE_STEP), jnp.float32),
            pltpu.VMEM((GROUPS * STRIDE, channels * width), jnp.float32),
            pltpu.VMEM(((rows + 2) * block, positions), jnp.bfloat16),
            pltpu.VMEM((count, each * width, positions), jnp.bfloat16),
            pltpu.VMEM((count, each * width, positions), jnp.bfloat16),
            pltpu.SemaphoreType.DMA((7,)),
            pltpu.SemaphoreType.DMA((count,)),
            pltpu.SemaphoreType.DMA((count,)),
        ],
        compiler_params=pltpu.CompilerParams(
            collective_id=0, has_side_effects=True, vmem_limit_bytes=60 * 1024 * 1024
        ),
        name="verify",
    )(
        round_owner,
        conv1_bias,
        conv2_bias,
        queries.reshape(maps * rows * width, depth),
        db_maps.reshape(positions, depth),
        taps_first(conv1_weight),
        taps_first(conv2_weight),
    )
    return result.reshape(rounds, 1, each, width, positions)


def solution(mesh):
    placed = (
        P(("groups", "qrow"), None, None, None),
        P(("groups", "db", "rep"), None, None),
        P("groups"),
        P(),
        P(),
        P(),
        P(),
    )
    return jax.shard_map(
        functools.partial(on_device, mesh.shape["qrow"]),
        mesh=mesh,
        in_specs=placed,
        out_specs=P(None, ("groups", "db", "rep"), "qrow", None, None),
        check_vma=False,
    )
```

```python
import functools
import math

import jax
import jax.numpy as jnp
from jax import lax
from jax.experimental import pallas as pl
from jax.experimental.pallas import tpu as pltpu
from jax.sharding import PartitionSpec as P

epsilon = 1e-05
TAPS = 9
SLOTS = 10
LANE_STEP = 256
STRIDE = 8
GROUPS = 28


def tap_row(a, b, c, d):
    return ((a * 3 + b) * 3 + c) * STRIDE + d


def tap_matrix(weight_ref, spread):
    groups, inner, channels = weight_ref.shape
    spread[pl.ds(0, groups), pl.ds(0, inner), :] = weight_ref[...].astype(jnp.float32)
    return spread[...].reshape(GROUPS * STRIDE, channels).astype(jnp.bfloat16)


def banded(masks, parts):
    value = jnp.zeros(masks[0].shape, jnp.float32)
    for mask, part in zip(masks, parts):
        value = jnp.where(mask, jnp.broadcast_to(part, mask.shape), value)
    return value


def fill_picks(width, pick_ref):
    rows = GROUPS * STRIDE
    block = SLOTS * width
    lane = lax.broadcasted_iota(jnp.int32, (1, LANE_STEP), 1)
    a = sum((lane >= k * block).astype(jnp.int32) for k in (1, 2))
    offset = lane - a * block
    tap = sum((offset >= k * width).astype(jnp.int32) for k in range(1, SLOTS))
    c = (tap >= 3).astype(jnp.int32) + (tap >= 6).astype(jnp.int32)
    d = tap - 3 * c
    valid = (tap < TAPS) & (lane < 3 * block)
    base = jnp.where(valid, tap_row(a, 0, c, d), -2 * rows)
    row = lax.broadcasted_iota(jnp.int32, (rows, LANE_STEP), 0)
    for b in range(3):
        pick_ref[b] = jnp.where(row == base + tap_row(0, b, 0, 0), 1.0, 0.0).astype(jnp.bfloat16)
    return offset - tap * width - lax.broadcasted_iota(jnp.int32, (width, LANE_STEP), 0) + 1


def first_matrix(taps, width, pick_ref, band, chosen_ref):
    for b in range(3):
        chosen_ref[b] = lax.dot_general(
            taps, pick_ref[b], (((0,), (0,)), ((), ())), preferred_element_type=jnp.float32
        )
    masks = [band == b for b in range(3)]
    return jnp.concatenate(
        [
            banded(masks, [chosen_ref[b, pl.ds(o, 1), :] for b in range(3)])
            for o in range(taps.shape[1])
        ],
        axis=0,
    ).astype(jnp.bfloat16)[:, : 3 * SLOTS * width]


def second_matrix(taps, width, wide_ref):
    channels = taps.shape[1]
    lanes = channels * width
    lane = lax.broadcasted_iota(jnp.int32, (channels, lanes), 1)
    start = lax.broadcasted_iota(jnp.int32, (channels, lanes), 0) * width
    repeat = jnp.where((lane >= start) & (lane < start + width), 1.0, 0.0).astype(jnp.bfloat16)
    wide_ref[...] = jnp.dot(taps, repeat, preferred_element_type=jnp.float32)
    channel = sum(
        (lax.broadcasted_iota(jnp.int32, (1, lanes), 1) >= k * width).astype(jnp.int32)
        for k in range(1, channels)
    )
    column = lax.broadcasted_iota(jnp.int32, (1, lanes), 1) - channel * width
    band = column - lax.broadcasted_iota(jnp.int32, (width, lanes), 0) + 1
    masks = [band == b for b in range(3)]
    return jnp.concatenate(
        [
            banded(masks, [wide_ref[pl.ds(tap_row(a, b, c, d), 1), :] for b in range(3)])
            for a in range(3)
            for c in range(3)
            for d in range(3)
        ],
        axis=0,
    ).astype(jnp.bfloat16)


def kernel(
    count,
    width,
    side,
    owner_hbm,
    bias1_hbm,
    query_hbm,
    map_hbm,
    weight1_hbm,
    weight2_hbm,
    out_ref,
    owner_ref,
    bias1_ref,
    query_ref,
    map_ref,
    weight1_ref,
    weight2_ref,
    spread1,
    spread2,
    pick,
    chosen,
    wide,
    shifted,
    result,
    received,
    load_sem,
    send_sem,
    recv_sem,
):
    loads = [
        pltpu.make_async_copy(source, target, load_sem.at[index])
        for index, (source, target) in enumerate(
            (
                (weight1_hbm, weight1_ref),
                (weight2_hbm, weight2_ref),
                (map_hbm, map_ref),
                (query_hbm, query_ref),
                (bias1_hbm, bias1_ref),
                (owner_hbm, owner_ref),
            )
        )
    ]
    for load in loads:
        load.start()
    me = lax.axis_index("qrow")
    barrier = pltpu.get_barrier_semaphore()
    for step in range(1, count):
        pl.semaphore_signal(
            barrier,
            inc=1,
            device_id={"qrow": lax.rem(me + step, count)},
            device_id_type=pl.DeviceIdType.MESH,
        )

    positions = map_ref.shape[0]
    rows = query_ref.shape[0] // width
    channels = weight1_ref.shape[2]
    block = SLOTS * width
    size = TAPS * width

    band = fill_picks(width, pick)
    for spread in (spread1, spread2):
        spread[...] = jnp.zeros_like(spread)
    blank = jnp.zeros((block, positions), jnp.bfloat16)
    shifted[pl.ds(0, block), :] = blank
    shifted[pl.ds((rows + 1) * block, block), :] = blank
    for load in loads:
        load.wait()

    matrix1 = first_matrix(tap_matrix(weight1_ref, spread1), width, pick, band, chosen)
    matrix2 = second_matrix(tap_matrix(weight2_ref, spread2), width, wide)

    corr = lax.dot_general(
        query_ref[...],
        map_ref[...],
        (((1,), (1,)), ((), ())),
        preferred_element_type=jnp.float32,
    ) * (1.0 / math.sqrt(query_ref.shape[1]))
    scores = jnp.maximum(corr, 0.0)
    col_scale = 1.0 / (jnp.max(scores, axis=0, keepdims=True) + epsilon)
    row_scale = 1.0 / (jnp.max(scores, axis=1, keepdims=True) + epsilon)
    mutual = scores * (scores * col_scale) * (scores * row_scale)

    lane = lax.broadcasted_iota(jnp.int32, (1, positions), 1)
    column = lane & (side - 1)

    def inner(value, d):
        if d == 1:
            return value
        moved = pltpu.roll(value, (1 - d) % positions, 1)
        return jnp.where(column == (0 if d == 0 else side - 1), 0.0, moved)

    def outer(value, c):
        if c == 1:
            return value
        moved = pltpu.roll(value, ((1 - c) * side) % positions, 1)
        edge = lane < side if c == 0 else lane >= positions - side
        return jnp.where(edge, 0.0, moved)

    along = [inner(mutual, d) for d in range(3)]
    taps = [outer(along[d], c) for c in range(3) for d in range(3)]
    gap = jnp.zeros((width, positions), jnp.float32)
    for i in range(rows):
        shifted[pl.ds((i + 1) * block, block), :] = jnp.concatenate(
            [tap[i * width : (i + 1) * width] for tap in taps] + [gap], axis=0
        ).astype(jnp.bfloat16)

    bias1 = jnp.concatenate(
        [jnp.full((width, positions), bias1_ref[o], jnp.float32) for o in range(channels)], axis=0
    )
    mixed = []
    for i in range(rows):
        hidden = jnp.dot(
            matrix1, shifted[pl.ds(i * block, 3 * block), :], preferred_element_type=jnp.float32
        )
        hidden = jnp.maximum(hidden + bias1, 0.0).astype(jnp.bfloat16)
        mixed.append(jnp.dot(matrix2, hidden, preferred_element_type=jnp.float32))

    each = rows // count
    for target in range(count):
        totals = []
        for i in range(target * each, (target + 1) * each):
            summed = mixed[i][size : 2 * size]
            if i > 0:
                summed = summed + mixed[i - 1][:size]
            if i < rows - 1:
                summed = summed + mixed[i + 1][2 * size :]
            total = None
            for c in range(3):
                row = None
                for d in range(3):
                    tap = (c * 3 + d) * width
                    term = inner(summed[tap : tap + width], d)
                    row = term if row is None else row + term
                row = outer(row, c)
                total = row if total is None else total + row
            totals.append(total)
        result[target] = jnp.concatenate(totals, axis=0)

    pl.semaphore_wait(barrier, count - 1)

    def transfer(source, target):
        return pltpu.make_async_remote_copy(
            src_ref=result.at[target],
            dst_ref=received.at[source],
            send_sem=send_sem.at[target],
            recv_sem=recv_sem.at[source],
            device_id={"qrow": target},
            device_id_type=pl.DeviceIdType.MESH,
        )

    for step in range(1, count):
        transfer(me, lax.rem(me + step, count)).start()
    received[me] = result[me]
    for step in range(1, count):
        transfer(lax.rem(me + step, count), me).wait_recv()
    for r in range(out_ref.shape[0]):
        out_ref[r] = received[owner_ref[r]]
    for step in range(1, count):
        transfer(me, lax.rem(me + step, count)).wait_send()


def on_device(count, queries, db_maps, round_owner, conv1_weight, conv1_bias, conv2_weight, conv2_bias):
    maps, rows, width, depth = queries.shape
    positions = db_maps.shape[1]
    channels = conv1_weight.shape[0]
    side = math.isqrt(positions)
    each = rows // count
    block = SLOTS * width
    rounds = round_owner.shape[0]

    def taps_first(weight):
        return jnp.transpose(weight, (1, 2, 3, 4, 0)).reshape(27, 3, channels)

    result = pl.pallas_call(
        functools.partial(kernel, count, width, side),
        out_shape=pltpu.VMEM((rounds, each * width, positions), jnp.float32),
        in_specs=[pl.BlockSpec(memory_space=pltpu.HBM)] * 6,
        out_specs=pl.BlockSpec(memory_space=pltpu.VMEM),
        scratch_shapes=[
            pltpu.SMEM((rounds,), jnp.int32),
            pltpu.SMEM((channels,), jnp.float32),
            pltpu.VMEM((rows * width, depth), jnp.bfloat16),
            pltpu.VMEM((positions, depth), jnp.bfloat16),
            pltpu.VMEM((27, 3, channels), jnp.bfloat16),
            pltpu.VMEM((27, 3, channels), jnp.bfloat16),
            pltpu.VMEM((GROUPS, STRIDE, channels), jnp.float32),
            pltpu.VMEM((GROUPS, STRIDE, channels), jnp.float32),
            pltpu.VMEM((3, GROUPS * STRIDE, LANE_STEP), jnp.bfloat16),
            pltpu.VMEM((3, channels, LANE_STEP), jnp.float32),
            pltpu.VMEM((GROUPS * STRIDE, channels * width), jnp.float32),
            pltpu.VMEM(((rows + 2) * block, positions), jnp.bfloat16),
            pltpu.VMEM((count, each * width, positions), jnp.float32),
            pltpu.VMEM((count, each * width, positions), jnp.float32),
            pltpu.SemaphoreType.DMA((6,)),
            pltpu.SemaphoreType.DMA((count,)),
            pltpu.SemaphoreType.DMA((count,)),
        ],
        compiler_params=pltpu.CompilerParams(
            collective_id=0, has_side_effects=True, vmem_limit_bytes=60 * 1024 * 1024
        ),
        name="verify",
    )(
        round_owner,
        conv1_bias,
        queries.reshape(maps * rows * width, depth),
        db_maps.reshape(positions, depth),
        taps_first(conv1_weight),
        taps_first(conv2_weight),
    )
    return jnp.maximum(result + conv2_bias[0], 0.0).reshape(rounds, 1, each, width, positions)


def solution(mesh):
    placed = (
        P(("groups", "qrow"), None, None, None),
        P(("groups", "db", "rep"), None, None),
        P("groups"),
        P(),
        P(),
        P(),
        P(),
    )
    return jax.shard_map(
        functools.partial(on_device, mesh.shape["qrow"]),
        mesh=mesh,
        in_specs=placed,
        out_specs=P(None, ("groups", "db", "rep"), "qrow", None, None),
        check_vma=False,
    )
```

```python
import functools
import math

import jax
import jax.numpy as jnp
from jax import lax
from jax.experimental import pallas as pl
from jax.experimental.pallas import tpu as pltpu
from jax.sharding import PartitionSpec as P

epsilon = 1e-05
TAPS = 9
SLOTS = 10
LANE_STEP = 256
STRIDE = 8
GROUPS = 28


def tap_row(a, b, c, d):
    return ((a * 3 + b) * 3 + c) * STRIDE + d


def tap_matrix(weight_ref, spread):
    groups, inner, channels = weight_ref.shape
    spread[pl.ds(0, groups), pl.ds(0, inner), :] = weight_ref[...].astype(jnp.float32)
    return spread[...].reshape(GROUPS * STRIDE, channels).astype(jnp.bfloat16)


def banded(masks, parts):
    value = jnp.zeros(masks[0].shape, jnp.float32)
    for mask, part in zip(masks, parts):
        value = jnp.where(mask, jnp.broadcast_to(part, mask.shape), value)
    return value


def fill_picks(width, pick_ref):
    rows = GROUPS * STRIDE
    block = SLOTS * width
    lane = lax.broadcasted_iota(jnp.int32, (1, LANE_STEP), 1)
    a = sum((lane >= k * block).astype(jnp.int32) for k in (1, 2))
    offset = lane - a * block
    tap = sum((offset >= k * width).astype(jnp.int32) for k in range(1, SLOTS))
    c = (tap >= 3).astype(jnp.int32) + (tap >= 6).astype(jnp.int32)
    d = tap - 3 * c
    valid = (tap < TAPS) & (lane < 3 * block)
    base = jnp.where(valid, tap_row(a, 0, c, d), -2 * rows)
    row = lax.broadcasted_iota(jnp.int32, (rows, LANE_STEP), 0)
    for b in range(3):
        pick_ref[b] = jnp.where(row == base + tap_row(0, b, 0, 0), 1.0, 0.0).astype(jnp.bfloat16)
    return offset - tap * width - lax.broadcasted_iota(jnp.int32, (width, LANE_STEP), 0) + 1


def first_matrix(taps, width, pick_ref, band, chosen_ref):
    for b in range(3):
        chosen_ref[b] = lax.dot_general(
            taps, pick_ref[b], (((0,), (0,)), ((), ())), preferred_element_type=jnp.float32
        )
    masks = [band == b for b in range(3)]
    return jnp.concatenate(
        [
            banded(masks, [chosen_ref[b, pl.ds(o, 1), :] for b in range(3)])
            for o in range(taps.shape[1])
        ],
        axis=0,
    ).astype(jnp.bfloat16)[:, : 3 * SLOTS * width]


def second_matrix(taps, width, wide_ref):
    channels = taps.shape[1]
    lanes = channels * width
    lane = lax.broadcasted_iota(jnp.int32, (channels, lanes), 1)
    start = lax.broadcasted_iota(jnp.int32, (channels, lanes), 0) * width
    repeat = jnp.where((lane >= start) & (lane < start + width), 1.0, 0.0).astype(jnp.bfloat16)
    wide_ref[...] = jnp.dot(taps, repeat, preferred_element_type=jnp.float32)
    channel = sum(
        (lax.broadcasted_iota(jnp.int32, (1, lanes), 1) >= k * width).astype(jnp.int32)
        for k in range(1, channels)
    )
    column = lax.broadcasted_iota(jnp.int32, (1, lanes), 1) - channel * width
    band = column - lax.broadcasted_iota(jnp.int32, (width, lanes), 0) + 1
    masks = [band == b for b in range(3)]
    return jnp.concatenate(
        [
            banded(masks, [wide_ref[pl.ds(tap_row(a, b, c, d), 1), :] for b in range(3)])
            for a in range(3)
            for c in range(3)
            for d in range(3)
        ],
        axis=0,
    ).astype(jnp.bfloat16)


def kernel(
    count,
    width,
    side,
    owner_hbm,
    bias1_hbm,
    query_hbm,
    map_hbm,
    weight1_hbm,
    weight2_hbm,
    out_ref,
    owner_ref,
    bias1_ref,
    query_ref,
    map_ref,
    weight1_ref,
    weight2_ref,
    spread1,
    spread2,
    pick,
    chosen,
    wide,
    shifted,
    result,
    received,
    load_sem,
    send_sem,
    recv_sem,
):
    loads = [
        pltpu.make_async_copy(source, target, load_sem.at[index])
        for index, (source, target) in enumerate(
            (
                (weight1_hbm, weight1_ref),
                (weight2_hbm, weight2_ref),
                (map_hbm, map_ref),
                (query_hbm, query_ref),
                (bias1_hbm, bias1_ref),
                (owner_hbm, owner_ref),
            )
        )
    ]
    for load in loads:
        load.start()
    me = lax.axis_index("qrow")
    barrier = pltpu.get_barrier_semaphore()
    for step in range(1, count):
        pl.semaphore_signal(
            barrier,
            inc=1,
            device_id={"qrow": lax.rem(me + step, count)},
            device_id_type=pl.DeviceIdType.MESH,
        )

    positions = map_ref.shape[0]
    rows = query_ref.shape[0] // width
    channels = weight1_ref.shape[2]
    block = SLOTS * width
    size = TAPS * width

    band = fill_picks(width, pick)
    for spread in (spread1, spread2):
        spread[...] = jnp.zeros_like(spread)
    blank = jnp.zeros((block, positions), jnp.bfloat16)
    shifted[pl.ds(0, block), :] = blank
    shifted[pl.ds((rows + 1) * block, block), :] = blank
    for load in loads:
        load.wait()

    matrix1 = first_matrix(tap_matrix(weight1_ref, spread1), width, pick, band, chosen)
    matrix2 = second_matrix(tap_matrix(weight2_ref, spread2), width, wide)

    corr = lax.dot_general(
        query_ref[...],
        map_ref[...],
        (((1,), (1,)), ((), ())),
        preferred_element_type=jnp.float32,
    ) * (1.0 / math.sqrt(query_ref.shape[1]))
    scores = jnp.maximum(corr, 0.0)
    col_scale = 1.0 / (jnp.max(scores, axis=0, keepdims=True) + epsilon)
    row_scale = 1.0 / (jnp.max(scores, axis=1, keepdims=True) + epsilon)
    mutual = scores * (scores * col_scale) * (scores * row_scale)

    lane = lax.broadcasted_iota(jnp.int32, (1, positions), 1)
    column = lane & (side - 1)

    def inner(value, d):
        if d == 1:
            return value
        moved = pltpu.roll(value, (1 - d) % positions, 1)
        return jnp.where(column == (0 if d == 0 else side - 1), 0.0, moved)

    def outer(value, c):
        if c == 1:
            return value
        moved = pltpu.roll(value, ((1 - c) * side) % positions, 1)
        edge = lane < side if c == 0 else lane >= positions - side
        return jnp.where(edge, 0.0, moved)

    along = [inner(mutual, d) for d in range(3)]
    taps = [outer(along[d], c) for c in range(3) for d in range(3)]
    gap = jnp.zeros((width, positions), jnp.float32)
    for i in range(rows):
        shifted[pl.ds((i + 1) * block, block), :] = jnp.concatenate(
            [tap[i * width : (i + 1) * width] for tap in taps] + [gap], axis=0
        ).astype(jnp.bfloat16)

    bias1 = jnp.concatenate(
        [jnp.full((width, positions), bias1_ref[o], jnp.float32) for o in range(channels)], axis=0
    )
    def transfer(source, target):
        return pltpu.make_async_remote_copy(
            src_ref=result.at[target],
            dst_ref=received.at[source],
            send_sem=send_sem.at[target],
            recv_sem=recv_sem.at[source],
            device_id={"qrow": target},
            device_id_type=pl.DeviceIdType.MESH,
        )

    pl.semaphore_wait(barrier, count - 1)
    mixed = []
    each = rows // count
    for target in range(count):
        for i in range(len(mixed), min((target + 1) * each + 1, rows)):
            hidden = jnp.dot(
                matrix1, shifted[pl.ds(i * block, 3 * block), :], preferred_element_type=jnp.float32
            )
            hidden = jnp.maximum(hidden + bias1, 0.0).astype(jnp.bfloat16)
            mixed.append(jnp.dot(matrix2, hidden, preferred_element_type=jnp.float32))
        totals = []
        for i in range(target * each, (target + 1) * each):
            summed = mixed[i][size : 2 * size]
            if i > 0:
                summed = summed + mixed[i - 1][:size]
            if i < rows - 1:
                summed = summed + mixed[i + 1][2 * size :]
            total = None
            for c in range(3):
                row = None
                for d in range(3):
                    tap = (c * 3 + d) * width
                    term = inner(summed[tap : tap + width], d)
                    row = term if row is None else row + term
                row = outer(row, c)
                total = row if total is None else total + row
            totals.append(total)
        result[target] = jnp.concatenate(totals, axis=0)

        @pl.when(target != me)
        def _():
            transfer(me, target).start()


    received[me] = result[me]
    for step in range(1, count):
        transfer(lax.rem(me + step, count), me).wait_recv()
    for r in range(out_ref.shape[0]):
        out_ref[r] = received[owner_ref[r]]
    for step in range(1, count):
        transfer(me, lax.rem(me + step, count)).wait_send()


def on_device(count, queries, db_maps, round_owner, conv1_weight, conv1_bias, conv2_weight, conv2_bias):
    maps, rows, width, depth = queries.shape
    positions = db_maps.shape[1]
    channels = conv1_weight.shape[0]
    side = math.isqrt(positions)
    each = rows // count
    block = SLOTS * width
    rounds = round_owner.shape[0]

    def taps_first(weight):
        return jnp.transpose(weight, (1, 2, 3, 4, 0)).reshape(27, 3, channels)

    result = pl.pallas_call(
        functools.partial(kernel, count, width, side),
        out_shape=pltpu.VMEM((rounds, each * width, positions), jnp.float32),
        in_specs=[pl.BlockSpec(memory_space=pltpu.HBM)] * 6,
        out_specs=pl.BlockSpec(memory_space=pltpu.VMEM),
        scratch_shapes=[
            pltpu.SMEM((rounds,), jnp.int32),
            pltpu.SMEM((channels,), jnp.float32),
            pltpu.VMEM((rows * width, depth), jnp.bfloat16),
            pltpu.VMEM((positions, depth), jnp.bfloat16),
            pltpu.VMEM((27, 3, channels), jnp.bfloat16),
            pltpu.VMEM((27, 3, channels), jnp.bfloat16),
            pltpu.VMEM((GROUPS, STRIDE, channels), jnp.float32),
            pltpu.VMEM((GROUPS, STRIDE, channels), jnp.float32),
            pltpu.VMEM((3, GROUPS * STRIDE, LANE_STEP), jnp.bfloat16),
            pltpu.VMEM((3, channels, LANE_STEP), jnp.float32),
            pltpu.VMEM((GROUPS * STRIDE, channels * width), jnp.float32),
            pltpu.VMEM(((rows + 2) * block, positions), jnp.bfloat16),
            pltpu.VMEM((count, each * width, positions), jnp.float32),
            pltpu.VMEM((count, each * width, positions), jnp.float32),
            pltpu.SemaphoreType.DMA((6,)),
            pltpu.SemaphoreType.DMA((count,)),
            pltpu.SemaphoreType.DMA((count,)),
        ],
        compiler_params=pltpu.CompilerParams(
            collective_id=0, has_side_effects=True, vmem_limit_bytes=60 * 1024 * 1024
        ),
        name="verify",
    )(
        round_owner,
        conv1_bias,
        queries.reshape(maps * rows * width, depth),
        db_maps.reshape(positions, depth),
        taps_first(conv1_weight),
        taps_first(conv2_weight),
    )
    return jnp.maximum(result + conv2_bias[0], 0.0).reshape(rounds, 1, each, width, positions)


def solution(mesh):
    placed = (
        P(("groups", "qrow"), None, None, None),
        P(("groups", "db", "rep"), None, None),
        P("groups"),
        P(),
        P(),
        P(),
        P(),
    )
    return jax.shard_map(
        functools.partial(on_device, mesh.shape["qrow"]),
        mesh=mesh,
        in_specs=placed,
        out_specs=P(None, ("groups", "db", "rep"), "qrow", None, None),
        check_vma=False,
    )
```

```python
import functools
import math

import jax
import jax.numpy as jnp
from jax import lax
from jax.experimental import pallas as pl
from jax.experimental.pallas import tpu as pltpu
from jax.sharding import PartitionSpec as P

epsilon = 1e-05
TAPS = 9
SLOTS = 10
LANE_STEP = 256
STRIDE = 8
GROUPS = 28


def tap_row(a, b, c, d):
    return ((a * 3 + b) * 3 + c) * STRIDE + d


def tap_matrix(weight_ref, spread):
    groups, inner, channels = weight_ref.shape
    spread[pl.ds(0, groups), pl.ds(0, inner), :] = weight_ref[...].astype(jnp.float32)
    return spread[...].reshape(GROUPS * STRIDE, channels).astype(jnp.bfloat16)


def banded(masks, parts):
    value = jnp.zeros(masks[0].shape, jnp.float32)
    for mask, part in zip(masks, parts):
        value = jnp.where(mask, jnp.broadcast_to(part, mask.shape), value)
    return value


def fill_picks(width, pick_ref):
    rows = GROUPS * STRIDE
    block = SLOTS * width
    lane = lax.broadcasted_iota(jnp.int32, (1, LANE_STEP), 1)
    a = sum((lane >= k * block).astype(jnp.int32) for k in (1, 2))
    offset = lane - a * block
    tap = sum((offset >= k * width).astype(jnp.int32) for k in range(1, SLOTS))
    c = (tap >= 3).astype(jnp.int32) + (tap >= 6).astype(jnp.int32)
    d = tap - 3 * c
    valid = (tap < TAPS) & (lane < 3 * block)
    base = jnp.where(valid, tap_row(a, 0, c, d), -2 * rows)
    row = lax.broadcasted_iota(jnp.int32, (rows, LANE_STEP), 0)
    for b in range(3):
        pick_ref[b] = jnp.where(row == base + tap_row(0, b, 0, 0), 1.0, 0.0).astype(jnp.bfloat16)
    return offset - tap * width - lax.broadcasted_iota(jnp.int32, (width, LANE_STEP), 0) + 1


def first_matrix(taps, width, pick_ref, band, chosen_ref):
    for b in range(3):
        chosen_ref[b] = lax.dot_general(
            taps, pick_ref[b], (((0,), (0,)), ((), ())), preferred_element_type=jnp.float32
        )
    masks = [band == b for b in range(3)]
    return jnp.concatenate(
        [
            banded(masks, [chosen_ref[b, pl.ds(o, 1), :] for b in range(3)])
            for o in range(taps.shape[1])
        ],
        axis=0,
    ).astype(jnp.bfloat16)[:, : 3 * SLOTS * width]


def second_matrix(taps, width, wide_ref):
    channels = taps.shape[1]
    lanes = channels * width
    lane = lax.broadcasted_iota(jnp.int32, (channels, lanes), 1)
    start = lax.broadcasted_iota(jnp.int32, (channels, lanes), 0) * width
    repeat = jnp.where((lane >= start) & (lane < start + width), 1.0, 0.0).astype(jnp.bfloat16)
    wide_ref[...] = jnp.dot(taps, repeat, preferred_element_type=jnp.float32)
    channel = sum(
        (lax.broadcasted_iota(jnp.int32, (1, lanes), 1) >= k * width).astype(jnp.int32)
        for k in range(1, channels)
    )
    column = lax.broadcasted_iota(jnp.int32, (1, lanes), 1) - channel * width
    band = column - lax.broadcasted_iota(jnp.int32, (width, lanes), 0) + 1
    masks = [band == b for b in range(3)]
    return jnp.concatenate(
        [
            banded(masks, [wide_ref[pl.ds(tap_row(a, b, c, d), 1), :] for b in range(3)])
            for a in range(3)
            for c in range(3)
            for d in range(3)
        ],
        axis=0,
    ).astype(jnp.bfloat16)


def kernel(
    count,
    width,
    side,
    owner_hbm,
    bias1_hbm,
    bias2_ref,
    query_hbm,
    map_hbm,
    weight1_hbm,
    weight2_hbm,
    out_ref,
    owner_ref,
    bias1_ref,
    query_ref,
    map_ref,
    weight1_ref,
    weight2_ref,
    spread1,
    spread2,
    pick,
    chosen,
    wide,
    shifted,
    result,
    received,
    load_sem,
    send_sem,
    recv_sem,
):
    loads = [
        pltpu.make_async_copy(source, target, load_sem.at[index])
        for index, (source, target) in enumerate(
            (
                (map_hbm, map_ref),
                (query_hbm, query_ref),
                (weight1_hbm, weight1_ref),
                (weight2_hbm, weight2_ref),
                (bias1_hbm, bias1_ref),
                (owner_hbm, owner_ref),
            )
        )
    ]
    for load in loads:
        load.start()
    me = lax.axis_index("qrow")
    barrier = pltpu.get_barrier_semaphore()
    for step in range(1, count):
        pl.semaphore_signal(
            barrier,
            inc=1,
            device_id={"qrow": lax.rem(me + step, count)},
            device_id_type=pl.DeviceIdType.MESH,
        )

    positions = map_ref.shape[0]
    rows = query_ref.shape[0] // width
    channels = weight1_ref.shape[2]
    block = SLOTS * width
    size = TAPS * width

    band = fill_picks(width, pick)
    for spread in (spread1, spread2):
        spread[...] = jnp.zeros_like(spread)
    blank = jnp.zeros((block, positions), jnp.bfloat16)
    shifted[pl.ds(0, block), :] = blank
    shifted[pl.ds((rows + 1) * block, block), :] = blank
    for load in loads:
        load.wait()

    matrix1 = first_matrix(tap_matrix(weight1_ref, spread1), width, pick, band, chosen)
    matrix2 = second_matrix(tap_matrix(weight2_ref, spread2), width, wide)

    corr = lax.dot_general(
        query_ref[...],
        map_ref[...],
        (((1,), (1,)), ((), ())),
        preferred_element_type=jnp.float32,
    ) * (1.0 / math.sqrt(query_ref.shape[1]))
    scores = jnp.maximum(corr, 0.0)
    col_scale = 1.0 / (jnp.max(scores, axis=0, keepdims=True) + epsilon)

    lane = lax.broadcasted_iota(jnp.int32, (1, positions), 1)
    column = lane & (side - 1)

    def inner(value, d):
        if d == 1:
            return value
        moved = pltpu.roll(value, (1 - d) % positions, 1)
        return jnp.where(column == (0 if d == 0 else side - 1), 0.0, moved)

    def outer(value, c):
        if c == 1:
            return value
        moved = pltpu.roll(value, ((1 - c) * side) % positions, 1)
        edge = lane < side if c == 0 else lane >= positions - side
        return jnp.where(edge, 0.0, moved)

    gap = jnp.zeros((width, positions), jnp.float32)

    def place(first, last):
        part = scores[first * width : last * width]
        row_scale = 1.0 / (jnp.max(part, axis=1, keepdims=True) + epsilon)
        mutual = part * (part * col_scale) * (part * row_scale)
        along = [inner(mutual, d) for d in range(3)]
        taps = [outer(along[d], c) for c in range(3) for d in range(3)]
        for i in range(first, last):
            start = (i - first) * width
            shifted[pl.ds((i + 1) * block, block), :] = jnp.concatenate(
                [tap[start : start + width] for tap in taps] + [gap], axis=0
            ).astype(jnp.bfloat16)

    bias1 = jnp.concatenate(
        [jnp.full((width, positions), bias1_ref[o], jnp.float32) for o in range(channels)], axis=0
    )
    def transfer(source, target):
        return pltpu.make_async_remote_copy(
            src_ref=result.at[target],
            dst_ref=received.at[source],
            send_sem=send_sem.at[target],
            recv_sem=recv_sem.at[source],
            device_id={"qrow": target},
            device_id_type=pl.DeviceIdType.MESH,
        )

    pl.semaphore_wait(barrier, count - 1)
    mixed = []
    placed = 0
    each = rows // count
    for target in range(count):
        needed = min((target + 1) * each + 2, rows)
        if needed > placed:
            place(placed, needed)
            placed = needed
        for i in range(len(mixed), min((target + 1) * each + 1, rows)):
            hidden = jnp.dot(
                matrix1, shifted[pl.ds(i * block, 3 * block), :], preferred_element_type=jnp.float32
            )
            hidden = jnp.maximum(hidden + bias1, 0.0).astype(jnp.bfloat16)
            mixed.append(jnp.dot(matrix2, hidden, preferred_element_type=jnp.float32))
        totals = []
        for i in range(target * each, (target + 1) * each):
            summed = mixed[i][size : 2 * size]
            if i > 0:
                summed = summed + mixed[i - 1][:size]
            if i < rows - 1:
                summed = summed + mixed[i + 1][2 * size :]
            total = None
            for c in range(3):
                row = None
                for d in range(3):
                    tap = (c * 3 + d) * width
                    term = inner(summed[tap : tap + width], d)
                    row = term if row is None else row + term
                row = outer(row, c)
                total = row if total is None else total + row
            totals.append(jnp.maximum(total + bias2_ref[0], 0.0))
        result[target] = jnp.concatenate(totals, axis=0).astype(jnp.bfloat16)

        @pl.when(target != me)
        def _():
            transfer(me, target).start()


    received[me] = result[me]
    for step in range(1, count):
        transfer(lax.rem(me + step, count), me).wait_recv()
    for r in range(out_ref.shape[0]):
        out_ref[r] = received[owner_ref[r]].astype(jnp.float32)
    for step in range(1, count):
        transfer(me, lax.rem(me + step, count)).wait_send()


def on_device(count, queries, db_maps, round_owner, conv1_weight, conv1_bias, conv2_weight, conv2_bias):
    maps, rows, width, depth = queries.shape
    positions = db_maps.shape[1]
    channels = conv1_weight.shape[0]
    side = math.isqrt(positions)
    each = rows // count
    block = SLOTS * width
    rounds = round_owner.shape[0]

    def taps_first(weight):
        return jnp.transpose(weight, (1, 2, 3, 4, 0)).reshape(27, 3, channels)

    result = pl.pallas_call(
        functools.partial(kernel, count, width, side),
        out_shape=pltpu.VMEM((rounds, each * width, positions), jnp.float32),
        in_specs=[pl.BlockSpec(memory_space=pltpu.HBM)] * 2
        + [pl.BlockSpec(memory_space=pltpu.SMEM)]
        + [pl.BlockSpec(memory_space=pltpu.HBM)] * 4,
        out_specs=pl.BlockSpec(memory_space=pltpu.VMEM),
        scratch_shapes=[
            pltpu.SMEM((rounds,), jnp.int32),
            pltpu.SMEM((channels,), jnp.float32),
            pltpu.VMEM((rows * width, depth), jnp.bfloat16),
            pltpu.VMEM((positions, depth), jnp.bfloat16),
            pltpu.VMEM((27, 3, channels), jnp.bfloat16),
            pltpu.VMEM((27, 3, channels), jnp.bfloat16),
            pltpu.VMEM((GROUPS, STRIDE, channels), jnp.float32),
            pltpu.VMEM((GROUPS, STRIDE, channels), jnp.float32),
            pltpu.VMEM((3, GROUPS * STRIDE, LANE_STEP), jnp.bfloat16),
            pltpu.VMEM((3, channels, LANE_STEP), jnp.float32),
            pltpu.VMEM((GROUPS * STRIDE, channels * width), jnp.float32),
            pltpu.VMEM(((rows + 2) * block, positions), jnp.bfloat16),
            pltpu.VMEM((count, each * width, positions), jnp.bfloat16),
            pltpu.VMEM((count, each * width, positions), jnp.bfloat16),
            pltpu.SemaphoreType.DMA((6,)),
            pltpu.SemaphoreType.DMA((count,)),
            pltpu.SemaphoreType.DMA((count,)),
        ],
        compiler_params=pltpu.CompilerParams(
            collective_id=0, has_side_effects=True, vmem_limit_bytes=60 * 1024 * 1024
        ),
        name="verify",
    )(
        round_owner,
        conv1_bias,
        conv2_bias,
        queries.reshape(maps * rows * width, depth),
        db_maps.reshape(positions, depth),
        taps_first(conv1_weight),
        taps_first(conv2_weight),
    )
    return result.reshape(rounds, 1, each, width, positions)


def solution(mesh):
    placed = (
        P(("groups", "qrow"), None, None, None),
        P(("groups", "db", "rep"), None, None),
        P("groups"),
        P(),
        P(),
        P(),
        P(),
    )
    return jax.shard_map(
        functools.partial(on_device, mesh.shape["qrow"]),
        mesh=mesh,
        in_specs=placed,
        out_specs=P(None, ("groups", "db", "rep"), "qrow", None, None),
        check_vma=False,
    )
```

```python
import functools
import math

import jax
import jax.numpy as jnp
from jax import lax
from jax.experimental import pallas as pl
from jax.experimental.pallas import tpu as pltpu
from jax.sharding import PartitionSpec as P

epsilon = 1e-05
TAPS = 9
SLOTS = 10
LANE_STEP = 256
STRIDE = 8
GROUPS = 28


def tap_row(a, b, c, d):
    return ((a * 3 + b) * 3 + c) * STRIDE + d


def tap_matrix(weight_ref, spread):
    groups, inner, channels = weight_ref.shape
    spread[pl.ds(0, groups), pl.ds(0, inner), :] = weight_ref[...].astype(jnp.float32)
    return spread[...].reshape(GROUPS * STRIDE, channels).astype(jnp.bfloat16)


def banded(masks, parts):
    value = jnp.zeros(masks[0].shape, jnp.float32)
    for mask, part in zip(masks, parts):
        value = jnp.where(mask, jnp.broadcast_to(part, mask.shape), value)
    return value


def band_rows(taps, width, wide_ref, backward, slots):
    channels = taps.shape[1]
    lanes = channels * width
    lane = lax.broadcasted_iota(jnp.int32, (channels, lanes), 1)
    start = lax.broadcasted_iota(jnp.int32, (channels, lanes), 0) * width
    repeat = jnp.where((lane >= start) & (lane < start + width), 1.0, 0.0).astype(jnp.bfloat16)
    wide_ref[...] = jnp.dot(taps, repeat, preferred_element_type=jnp.float32)
    channel = sum(
        (lax.broadcasted_iota(jnp.int32, (1, lanes), 1) >= k * width).astype(jnp.int32)
        for k in range(1, channels)
    )
    column = lax.broadcasted_iota(jnp.int32, (1, lanes), 1) - channel * width
    band = column - lax.broadcasted_iota(jnp.int32, (width, lanes), 0)
    masks = [band == ((1 - b) if backward else (b - 1)) for b in range(3)]
    pieces = []
    for a in range(3):
        for c in range(3):
            for d in range(3):
                pieces.append(
                    banded(masks, [wide_ref[pl.ds(tap_row(a, b, c, d), 1), :] for b in range(3)])
                )
        if slots > TAPS:
            pieces.append(jnp.zeros(((slots - TAPS) * width, lanes), jnp.float32))
    return jnp.concatenate(pieces, axis=0)


def kernel(
    count,
    width,
    side,
    owner_hbm,
    bias1_hbm,
    query_hbm,
    map_hbm,
    weight1_hbm,
    weight2_hbm,
    out_ref,
    owner_ref,
    bias1_ref,
    query_ref,
    map_ref,
    weight1_ref,
    weight2_ref,
    spread1,
    spread2,
    wide1,
    wide2,
    shifted,
    result,
    received,
    load_sem,
    send_sem,
    recv_sem,
):
    loads = [
        pltpu.make_async_copy(source, target, load_sem.at[index])
        for index, (source, target) in enumerate(
            (
                (weight1_hbm, weight1_ref),
                (weight2_hbm, weight2_ref),
                (map_hbm, map_ref),
                (query_hbm, query_ref),
                (bias1_hbm, bias1_ref),
                (owner_hbm, owner_ref),
            )
        )
    ]
    for load in loads:
        load.start()
    me = lax.axis_index("qrow")
    barrier = pltpu.get_barrier_semaphore()
    for step in range(1, count):
        pl.semaphore_signal(
            barrier,
            inc=1,
            device_id={"qrow": lax.rem(me + step, count)},
            device_id_type=pl.DeviceIdType.MESH,
        )

    positions = map_ref.shape[0]
    rows = query_ref.shape[0] // width
    channels = weight1_ref.shape[2]
    block = SLOTS * width
    size = TAPS * width

    for spread in (spread1, spread2):
        spread[...] = jnp.zeros_like(spread)
    blank = jnp.zeros((block, positions), jnp.bfloat16)
    shifted[pl.ds(0, block), :] = blank
    shifted[pl.ds((rows + 1) * block, block), :] = blank
    for load in loads:
        load.wait()

    tall = band_rows(tap_matrix(weight1_ref, spread1), width, wide1, True, SLOTS)
    spare = jnp.zeros((LANE_STEP - tall.shape[0], tall.shape[1]), jnp.float32)
    matrix1 = jnp.concatenate([tall, spare], axis=0).T.astype(jnp.bfloat16)[:, : 3 * block]
    matrix2 = band_rows(tap_matrix(weight2_ref, spread2), width, wide2, False, TAPS).astype(
        jnp.bfloat16
    )

    corr = lax.dot_general(
        query_ref[...],
        map_ref[...],
        (((1,), (1,)), ((), ())),
        preferred_element_type=jnp.float32,
    ) * (1.0 / math.sqrt(query_ref.shape[1]))
    scores = jnp.maximum(corr, 0.0)
    col_scale = 1.0 / (jnp.max(scores, axis=0, keepdims=True) + epsilon)
    row_scale = 1.0 / (jnp.max(scores, axis=1, keepdims=True) + epsilon)
    mutual = scores * (scores * col_scale) * (scores * row_scale)

    lane = lax.broadcasted_iota(jnp.int32, (1, positions), 1)
    column = lane & (side - 1)

    def inner(value, d):
        if d == 1:
            return value
        moved = pltpu.roll(value, (1 - d) % positions, 1)
        return jnp.where(column == (0 if d == 0 else side - 1), 0.0, moved)

    def outer(value, c):
        if c == 1:
            return value
        moved = pltpu.roll(value, ((1 - c) * side) % positions, 1)
        edge = lane < side if c == 0 else lane >= positions - side
        return jnp.where(edge, 0.0, moved)

    along = [inner(mutual, d) for d in range(3)]
    taps = [outer(along[d], c) for c in range(3) for d in range(3)]
    gap = jnp.zeros((width, positions), jnp.float32)
    for i in range(rows):
        shifted[pl.ds((i + 1) * block, block), :] = jnp.concatenate(
            [tap[i * width : (i + 1) * width] for tap in taps] + [gap], axis=0
        ).astype(jnp.bfloat16)

    bias1 = jnp.concatenate(
        [jnp.full((width, positions), bias1_ref[o], jnp.float32) for o in range(channels)], axis=0
    )
    def transfer(source, target):
        return pltpu.make_async_remote_copy(
            src_ref=result.at[target],
            dst_ref=received.at[source],
            send_sem=send_sem.at[target],
            recv_sem=recv_sem.at[source],
            device_id={"qrow": target},
            device_id_type=pl.DeviceIdType.MESH,
        )

    pl.semaphore_wait(barrier, count - 1)
    mixed = []
    each = rows // count
    for target in range(count):
        for i in range(len(mixed), min((target + 1) * each + 1, rows)):
            hidden = jnp.dot(
                matrix1, shifted[pl.ds(i * block, 3 * block), :], preferred_element_type=jnp.float32
            )
            hidden = jnp.maximum(hidden + bias1, 0.0).astype(jnp.bfloat16)
            mixed.append(jnp.dot(matrix2, hidden, preferred_element_type=jnp.float32))
        totals = []
        for i in range(target * each, (target + 1) * each):
            summed = mixed[i][size : 2 * size]
            if i > 0:
                summed = summed + mixed[i - 1][:size]
            if i < rows - 1:
                summed = summed + mixed[i + 1][2 * size :]
            total = None
            for c in range(3):
                row = None
                for d in range(3):
                    tap = (c * 3 + d) * width
                    term = inner(summed[tap : tap + width], d)
                    row = term if row is None else row + term
                row = outer(row, c)
                total = row if total is None else total + row
            totals.append(total)
        result[target] = jnp.concatenate(totals, axis=0)

        @pl.when(target != me)
        def _():
            transfer(me, target).start()


    received[me] = result[me]
    for step in range(1, count):
        transfer(lax.rem(me + step, count), me).wait_recv()
    for r in range(out_ref.shape[0]):
        out_ref[r] = received[owner_ref[r]]
    for step in range(1, count):
        transfer(me, lax.rem(me + step, count)).wait_send()


def on_device(count, queries, db_maps, round_owner, conv1_weight, conv1_bias, conv2_weight, conv2_bias):
    maps, rows, width, depth = queries.shape
    positions = db_maps.shape[1]
    channels = conv1_weight.shape[0]
    side = math.isqrt(positions)
    each = rows // count
    block = SLOTS * width
    rounds = round_owner.shape[0]

    def taps_first(weight):
        return jnp.transpose(weight, (1, 2, 3, 4, 0)).reshape(27, 3, channels)

    result = pl.pallas_call(
        functools.partial(kernel, count, width, side),
        out_shape=pltpu.VMEM((rounds, each * width, positions), jnp.float32),
        in_specs=[pl.BlockSpec(memory_space=pltpu.HBM)] * 6,
        out_specs=pl.BlockSpec(memory_space=pltpu.VMEM),
        scratch_shapes=[
            pltpu.SMEM((rounds,), jnp.int32),
            pltpu.SMEM((channels,), jnp.float32),
            pltpu.VMEM((rows * width, depth), jnp.bfloat16),
            pltpu.VMEM((positions, depth), jnp.bfloat16),
            pltpu.VMEM((27, 3, channels), jnp.bfloat16),
            pltpu.VMEM((27, 3, channels), jnp.bfloat16),
            pltpu.VMEM((GROUPS, STRIDE, channels), jnp.float32),
            pltpu.VMEM((GROUPS, STRIDE, channels), jnp.float32),
            pltpu.VMEM((GROUPS * STRIDE, channels * width), jnp.float32),
            pltpu.VMEM((GROUPS * STRIDE, channels * width), jnp.float32),
            pltpu.VMEM(((rows + 2) * block, positions), jnp.bfloat16),
            pltpu.VMEM((count, each * width, positions), jnp.float32),
            pltpu.VMEM((count, each * width, positions), jnp.float32),
            pltpu.SemaphoreType.DMA((6,)),
            pltpu.SemaphoreType.DMA((count,)),
            pltpu.SemaphoreType.DMA((count,)),
        ],
        compiler_params=pltpu.CompilerParams(
            collective_id=0, has_side_effects=True, vmem_limit_bytes=60 * 1024 * 1024
        ),
        name="verify",
    )(
        round_owner,
        conv1_bias,
        queries.reshape(maps * rows * width, depth),
        db_maps.reshape(positions, depth),
        taps_first(conv1_weight),
        taps_first(conv2_weight),
    )
    return jnp.maximum(result + conv2_bias[0], 0.0).reshape(rounds, 1, each, width, positions)


def solution(mesh):
    placed = (
        P(("groups", "qrow"), None, None, None),
        P(("groups", "db", "rep"), None, None),
        P("groups"),
        P(),
        P(),
        P(),
        P(),
    )
    return jax.shard_map(
        functools.partial(on_device, mesh.shape["qrow"]),
        mesh=mesh,
        in_specs=placed,
        out_specs=P(None, ("groups", "db", "rep"), "qrow", None, None),
        check_vma=False,
    )
```

```python
import functools
import math

import jax
import jax.numpy as jnp
from jax import lax
from jax.experimental import pallas as pl
from jax.experimental.pallas import tpu as pltpu
from jax.sharding import PartitionSpec as P

epsilon = 1e-05
TAPS = 9
SLOTS = 10
LANE_STEP = 256
STRIDE = 8
GROUPS = 28


def tap_row(a, b, c, d):
    return ((a * 3 + b) * 3 + c) * STRIDE + d


def tap_matrix(weight_ref, spread):
    groups, inner, channels = weight_ref.shape
    spread[pl.ds(0, groups), pl.ds(0, inner), :] = weight_ref[...].astype(jnp.float32)
    return spread[...].reshape(GROUPS * STRIDE, channels).astype(jnp.bfloat16)


def banded(masks, parts):
    value = jnp.zeros(masks[0].shape, jnp.float32)
    for mask, part in zip(masks, parts):
        value = jnp.where(mask, jnp.broadcast_to(part, mask.shape), value)
    return value


def band_rows(taps, width, wide_ref, backward, slots):
    channels = taps.shape[1]
    lanes = channels * width
    lane = lax.broadcasted_iota(jnp.int32, (channels, lanes), 1)
    start = lax.broadcasted_iota(jnp.int32, (channels, lanes), 0) * width
    repeat = jnp.where((lane >= start) & (lane < start + width), 1.0, 0.0).astype(jnp.bfloat16)
    wide_ref[...] = jnp.dot(taps, repeat, preferred_element_type=jnp.float32)
    channel = sum(
        (lax.broadcasted_iota(jnp.int32, (1, lanes), 1) >= k * width).astype(jnp.int32)
        for k in range(1, channels)
    )
    column = lax.broadcasted_iota(jnp.int32, (1, lanes), 1) - channel * width
    band = column - lax.broadcasted_iota(jnp.int32, (width, lanes), 0)
    masks = [band == ((1 - b) if backward else (b - 1)) for b in range(3)]
    pieces = []
    for a in range(3):
        for c in range(3):
            for d in range(3):
                pieces.append(
                    banded(masks, [wide_ref[pl.ds(tap_row(a, b, c, d), 1), :] for b in range(3)])
                )
        if slots > TAPS:
            pieces.append(jnp.zeros(((slots - TAPS) * width, lanes), jnp.float32))
    return jnp.concatenate(pieces, axis=0)


def kernel(
    count,
    width,
    side,
    owner_hbm,
    bias1_hbm,
    query_hbm,
    map_hbm,
    weight1_hbm,
    weight2_hbm,
    out_ref,
    owner_ref,
    bias1_ref,
    query_ref,
    map_ref,
    weight1_ref,
    weight2_ref,
    spread1,
    spread2,
    wide1,
    wide2,
    shifted,
    result,
    received,
    load_sem,
    send_sem,
    recv_sem,
):
    loads = [
        pltpu.make_async_copy(source, target, load_sem.at[index])
        for index, (source, target) in enumerate(
            (
                (weight1_hbm, weight1_ref),
                (weight2_hbm, weight2_ref),
                (map_hbm, map_ref),
                (query_hbm, query_ref),
                (bias1_hbm, bias1_ref),
                (owner_hbm, owner_ref),
            )
        )
    ]
    for load in loads:
        load.start()
    me = lax.axis_index("qrow")
    barrier = pltpu.get_barrier_semaphore()
    for step in range(1, count):
        pl.semaphore_signal(
            barrier,
            inc=1,
            device_id={"qrow": lax.rem(me + step, count)},
            device_id_type=pl.DeviceIdType.MESH,
        )

    positions = map_ref.shape[0]
    rows = query_ref.shape[0] // width
    channels = weight1_ref.shape[2]
    block = SLOTS * width
    size = TAPS * width

    for spread in (spread1, spread2):
        spread[...] = jnp.zeros_like(spread)
    blank = jnp.zeros((block, positions), jnp.bfloat16)
    shifted[pl.ds(0, block), :] = blank
    shifted[pl.ds((rows + 1) * block, block), :] = blank
    for load in loads:
        load.wait()

    tall = band_rows(tap_matrix(weight1_ref, spread1), width, wide1, True, SLOTS)
    spare = jnp.zeros((LANE_STEP - tall.shape[0], tall.shape[1]), jnp.float32)
    matrix1 = jnp.concatenate([tall, spare], axis=0).T.astype(jnp.bfloat16)[:, : 3 * block]
    matrix2 = band_rows(tap_matrix(weight2_ref, spread2), width, wide2, False, TAPS).astype(
        jnp.bfloat16
    )

    corr = lax.dot_general(
        map_ref[...],
        query_ref[...],
        (((1,), (1,)), ((), ())),
        preferred_element_type=jnp.float32,
    ) * (1.0 / math.sqrt(query_ref.shape[1]))
    scores = jnp.maximum(corr.T, 0.0)
    col_scale = 1.0 / (jnp.max(scores, axis=0, keepdims=True) + epsilon)
    row_scale = 1.0 / (jnp.max(scores, axis=1, keepdims=True) + epsilon)
    mutual = scores * (scores * col_scale) * (scores * row_scale)

    lane = lax.broadcasted_iota(jnp.int32, (1, positions), 1)
    column = lane & (side - 1)

    def inner(value, d):
        if d == 1:
            return value
        moved = pltpu.roll(value, (1 - d) % positions, 1)
        return jnp.where(column == (0 if d == 0 else side - 1), 0.0, moved)

    def outer(value, c):
        if c == 1:
            return value
        moved = pltpu.roll(value, ((1 - c) * side) % positions, 1)
        edge = lane < side if c == 0 else lane >= positions - side
        return jnp.where(edge, 0.0, moved)

    along = [inner(mutual, d) for d in range(3)]
    taps = [outer(along[d], c) for c in range(3) for d in range(3)]
    gap = jnp.zeros((width, positions), jnp.float32)
    for i in range(rows):
        shifted[pl.ds((i + 1) * block, block), :] = jnp.concatenate(
            [tap[i * width : (i + 1) * width] for tap in taps] + [gap], axis=0
        ).astype(jnp.bfloat16)

    bias1 = jnp.concatenate(
        [jnp.full((width, positions), bias1_ref[o], jnp.float32) for o in range(channels)], axis=0
    )
    def transfer(source, target):
        return pltpu.make_async_remote_copy(
            src_ref=result.at[target],
            dst_ref=received.at[source],
            send_sem=send_sem.at[target],
            recv_sem=recv_sem.at[source],
            device_id={"qrow": target},
            device_id_type=pl.DeviceIdType.MESH,
        )

    pl.semaphore_wait(barrier, count - 1)
    mixed = []
    each = rows // count
    for target in range(count):
        for i in range(len(mixed), min((target + 1) * each + 1, rows)):
            hidden = jnp.dot(
                matrix1, shifted[pl.ds(i * block, 3 * block), :], preferred_element_type=jnp.float32
            )
            hidden = jnp.maximum(hidden + bias1, 0.0).astype(jnp.bfloat16)
            mixed.append(jnp.dot(matrix2, hidden, preferred_element_type=jnp.float32))
        totals = []
        for i in range(target * each, (target + 1) * each):
            summed = mixed[i][size : 2 * size]
            if i > 0:
                summed = summed + mixed[i - 1][:size]
            if i < rows - 1:
                summed = summed + mixed[i + 1][2 * size :]
            total = None
            for c in range(3):
                row = None
                for d in range(3):
                    tap = (c * 3 + d) * width
                    term = inner(summed[tap : tap + width], d)
                    row = term if row is None else row + term
                row = outer(row, c)
                total = row if total is None else total + row
            totals.append(total)
        result[target] = jnp.concatenate(totals, axis=0)

        @pl.when(target != me)
        def _():
            transfer(me, target).start()


    received[me] = result[me]
    for step in range(1, count):
        transfer(lax.rem(me + step, count), me).wait_recv()
    for r in range(out_ref.shape[0]):
        out_ref[r] = received[owner_ref[r]]
    for step in range(1, count):
        transfer(me, lax.rem(me + step, count)).wait_send()


def on_device(count, queries, db_maps, round_owner, conv1_weight, conv1_bias, conv2_weight, conv2_bias):
    maps, rows, width, depth = queries.shape
    positions = db_maps.shape[1]
    channels = conv1_weight.shape[0]
    side = math.isqrt(positions)
    each = rows // count
    block = SLOTS * width
    rounds = round_owner.shape[0]

    def taps_first(weight):
        return jnp.transpose(weight, (1, 2, 3, 4, 0)).reshape(27, 3, channels)

    result = pl.pallas_call(
        functools.partial(kernel, count, width, side),
        out_shape=pltpu.VMEM((rounds, each * width, positions), jnp.float32),
        in_specs=[pl.BlockSpec(memory_space=pltpu.HBM)] * 6,
        out_specs=pl.BlockSpec(memory_space=pltpu.VMEM),
        scratch_shapes=[
            pltpu.SMEM((rounds,), jnp.int32),
            pltpu.SMEM((channels,), jnp.float32),
            pltpu.VMEM((rows * width, depth), jnp.bfloat16),
            pltpu.VMEM((positions, depth), jnp.bfloat16),
            pltpu.VMEM((27, 3, channels), jnp.bfloat16),
            pltpu.VMEM((27, 3, channels), jnp.bfloat16),
            pltpu.VMEM((GROUPS, STRIDE, channels), jnp.float32),
            pltpu.VMEM((GROUPS, STRIDE, channels), jnp.float32),
            pltpu.VMEM((GROUPS * STRIDE, channels * width), jnp.float32),
            pltpu.VMEM((GROUPS * STRIDE, channels * width), jnp.float32),
            pltpu.VMEM(((rows + 2) * block, positions), jnp.bfloat16),
            pltpu.VMEM((count, each * width, positions), jnp.float32),
            pltpu.VMEM((count, each * width, positions), jnp.float32),
            pltpu.SemaphoreType.DMA((6,)),
            pltpu.SemaphoreType.DMA((count,)),
            pltpu.SemaphoreType.DMA((count,)),
        ],
        compiler_params=pltpu.CompilerParams(
            collective_id=0, has_side_effects=True, vmem_limit_bytes=60 * 1024 * 1024
        ),
        name="verify",
    )(
        round_owner,
        conv1_bias,
        queries.reshape(maps * rows * width, depth),
        db_maps.reshape(positions, depth),
        taps_first(conv1_weight),
        taps_first(conv2_weight),
    )
    return jnp.maximum(result + conv2_bias[0], 0.0).reshape(rounds, 1, each, width, positions)


def solution(mesh):
    placed = (
        P(("groups", "qrow"), None, None, None),
        P(("groups", "db", "rep"), None, None),
        P("groups"),
        P(),
        P(),
        P(),
        P(),
    )
    return jax.shard_map(
        functools.partial(on_device, mesh.shape["qrow"]),
        mesh=mesh,
        in_specs=placed,
        out_specs=P(None, ("groups", "db", "rep"), "qrow", None, None),
        check_vma=False,
    )
```

```python
import functools
import math

import jax
import jax.numpy as jnp
from jax import lax
from jax.experimental import pallas as pl
from jax.experimental.pallas import tpu as pltpu
from jax.sharding import PartitionSpec as P

epsilon = 1e-05
TAPS = 9
SLOTS = 10
LANE_STEP = 256
STRIDE = 8
GROUPS = 28


def tap_row(a, b, c, d):
    return ((a * 3 + b) * 3 + c) * STRIDE + d


def tap_matrix(weight_ref, spread):
    groups, inner, channels = weight_ref.shape
    spread[pl.ds(0, groups), pl.ds(0, inner), :] = weight_ref[...].astype(jnp.float32)
    return spread[...].reshape(GROUPS * STRIDE, channels).astype(jnp.bfloat16)


def banded(masks, parts):
    value = jnp.zeros(masks[0].shape, jnp.float32)
    for mask, part in zip(masks, parts):
        value = jnp.where(mask, jnp.broadcast_to(part, mask.shape), value)
    return value


def band_rows(taps, width, wide_ref, backward, slots):
    channels = taps.shape[1]
    lanes = channels * width
    lane = lax.broadcasted_iota(jnp.int32, (channels, lanes), 1)
    start = lax.broadcasted_iota(jnp.int32, (channels, lanes), 0) * width
    repeat = jnp.where((lane >= start) & (lane < start + width), 1.0, 0.0).astype(jnp.bfloat16)
    wide_ref[...] = jnp.dot(taps, repeat, preferred_element_type=jnp.float32)
    channel = sum(
        (lax.broadcasted_iota(jnp.int32, (1, lanes), 1) >= k * width).astype(jnp.int32)
        for k in range(1, channels)
    )
    column = lax.broadcasted_iota(jnp.int32, (1, lanes), 1) - channel * width
    band = column - lax.broadcasted_iota(jnp.int32, (width, lanes), 0)
    masks = [band == ((1 - b) if backward else (b - 1)) for b in range(3)]
    pieces = []
    for a in range(3):
        for c in range(3):
            for d in range(3):
                pieces.append(
                    banded(masks, [wide_ref[pl.ds(tap_row(a, b, c, d), 1), :] for b in range(3)])
                )
        if slots > TAPS:
            pieces.append(jnp.zeros(((slots - TAPS) * width, lanes), jnp.float32))
    return jnp.concatenate(pieces, axis=0)


def kernel(
    count,
    width,
    side,
    owner_hbm,
    bias1_hbm,
    query_hbm,
    map_hbm,
    weight1_hbm,
    weight2_hbm,
    out_ref,
    owner_ref,
    bias1_ref,
    query_ref,
    map_ref,
    weight1_ref,
    weight2_ref,
    spread1,
    spread2,
    wide1,
    wide2,
    shifted,
    result,
    received,
    load_sem,
    send_sem,
    recv_sem,
):
    loads = [
        pltpu.make_async_copy(source, target, load_sem.at[index])
        for index, (source, target) in enumerate(
            (
                (map_hbm, map_ref),
                (query_hbm, query_ref),
                (weight1_hbm, weight1_ref),
                (weight2_hbm, weight2_ref),
                (bias1_hbm, bias1_ref),
                (owner_hbm, owner_ref),
            )
        )
    ]
    for load in loads:
        load.start()
    me = lax.axis_index("qrow")
    barrier = pltpu.get_barrier_semaphore()
    for step in range(1, count):
        pl.semaphore_signal(
            barrier,
            inc=1,
            device_id={"qrow": lax.rem(me + step, count)},
            device_id_type=pl.DeviceIdType.MESH,
        )

    positions = map_ref.shape[0]
    rows = query_ref.shape[0] // width
    channels = weight1_ref.shape[2]
    block = SLOTS * width
    size = TAPS * width

    for spread in (spread1, spread2):
        spread[...] = jnp.zeros_like(spread)
    blank = jnp.zeros((block, positions), jnp.bfloat16)
    shifted[pl.ds(0, block), :] = blank
    shifted[pl.ds((rows + 1) * block, block), :] = blank
    for load in loads:
        load.wait()

    tall = band_rows(tap_matrix(weight1_ref, spread1), width, wide1, True, SLOTS)
    spare = jnp.zeros((LANE_STEP - tall.shape[0], tall.shape[1]), jnp.float32)
    matrix1 = jnp.concatenate([tall, spare], axis=0).T.astype(jnp.bfloat16)[:, : 3 * block]
    matrix2 = band_rows(tap_matrix(weight2_ref, spread2), width, wide2, False, TAPS).astype(
        jnp.bfloat16
    )

    corr = lax.dot_general(
        query_ref[...],
        map_ref[...],
        (((1,), (1,)), ((), ())),
        preferred_element_type=jnp.float32,
    ) * (1.0 / math.sqrt(query_ref.shape[1]))
    scores = jnp.maximum(corr, 0.0)
    col_scale = 1.0 / (jnp.max(scores, axis=0, keepdims=True) + epsilon)

    lane = lax.broadcasted_iota(jnp.int32, (1, positions), 1)
    column = lane & (side - 1)

    def inner(value, d):
        if d == 1:
            return value
        moved = pltpu.roll(value, (1 - d) % positions, 1)
        return jnp.where(column == (0 if d == 0 else side - 1), 0.0, moved)

    def outer(value, c):
        if c == 1:
            return value
        moved = pltpu.roll(value, ((1 - c) * side) % positions, 1)
        edge = lane < side if c == 0 else lane >= positions - side
        return jnp.where(edge, 0.0, moved)

    gap = jnp.zeros((width, positions), jnp.float32)

    def place(first, last):
        part = scores[first * width : last * width]
        row_scale = 1.0 / (jnp.max(part, axis=1, keepdims=True) + epsilon)
        mutual = part * (part * col_scale) * (part * row_scale)
        along = [inner(mutual, d) for d in range(3)]
        taps = [outer(along[d], c) for c in range(3) for d in range(3)]
        for i in range(first, last):
            start = (i - first) * width
            shifted[pl.ds((i + 1) * block, block), :] = jnp.concatenate(
                [tap[start : start + width] for tap in taps] + [gap], axis=0
            ).astype(jnp.bfloat16)

    bias1 = jnp.concatenate(
        [jnp.full((width, positions), bias1_ref[o], jnp.float32) for o in range(channels)], axis=0
    )
    def transfer(source, target):
        return pltpu.make_async_remote_copy(
            src_ref=result.at[target],
            dst_ref=received.at[source],
            send_sem=send_sem.at[target],
            recv_sem=recv_sem.at[source],
            device_id={"qrow": target},
            device_id_type=pl.DeviceIdType.MESH,
        )

    pl.semaphore_wait(barrier, count - 1)
    mixed = []
    placed = 0
    each = rows // count
    for target in range(count):
        needed = min((target + 1) * each + 2, rows)
        if needed > placed:
            place(placed, needed)
            placed = needed
        for i in range(len(mixed), min((target + 1) * each + 1, rows)):
            hidden = jnp.dot(
                matrix1, shifted[pl.ds(i * block, 3 * block), :], preferred_element_type=jnp.float32
            )
            hidden = jnp.maximum(hidden + bias1, 0.0).astype(jnp.bfloat16)
            mixed.append(jnp.dot(matrix2, hidden, preferred_element_type=jnp.float32))
        totals = []
        for i in range(target * each, (target + 1) * each):
            summed = mixed[i][size : 2 * size]
            if i > 0:
                summed = summed + mixed[i - 1][:size]
            if i < rows - 1:
                summed = summed + mixed[i + 1][2 * size :]
            total = None
            for c in range(3):
                row = None
                for d in range(3):
                    tap = (c * 3 + d) * width
                    term = inner(summed[tap : tap + width], d)
                    row = term if row is None else row + term
                row = outer(row, c)
                total = row if total is None else total + row
            totals.append(total)
        result[target] = jnp.concatenate(totals, axis=0)

        @pl.when(target != me)
        def _():
            transfer(me, target).start()


    received[me] = result[me]
    for step in range(1, count):
        transfer(lax.rem(me + step, count), me).wait_recv()
    for r in range(out_ref.shape[0]):
        out_ref[r] = received[owner_ref[r]]
    for step in range(1, count):
        transfer(me, lax.rem(me + step, count)).wait_send()


def on_device(count, queries, db_maps, round_owner, conv1_weight, conv1_bias, conv2_weight, conv2_bias):
    maps, rows, width, depth = queries.shape
    positions = db_maps.shape[1]
    channels = conv1_weight.shape[0]
    side = math.isqrt(positions)
    each = rows // count
    block = SLOTS * width
    rounds = round_owner.shape[0]

    def taps_first(weight):
        return jnp.transpose(weight, (1, 2, 3, 4, 0)).reshape(27, 3, channels)

    result = pl.pallas_call(
        functools.partial(kernel, count, width, side),
        out_shape=pltpu.VMEM((rounds, each * width, positions), jnp.float32),
        in_specs=[pl.BlockSpec(memory_space=pltpu.HBM)] * 6,
        out_specs=pl.BlockSpec(memory_space=pltpu.VMEM),
        scratch_shapes=[
            pltpu.SMEM((rounds,), jnp.int32),
            pltpu.SMEM((channels,), jnp.float32),
            pltpu.VMEM((rows * width, depth), jnp.bfloat16),
            pltpu.VMEM((positions, depth), jnp.bfloat16),
            pltpu.VMEM((27, 3, channels), jnp.bfloat16),
            pltpu.VMEM((27, 3, channels), jnp.bfloat16),
            pltpu.VMEM((GROUPS, STRIDE, channels), jnp.float32),
            pltpu.VMEM((GROUPS, STRIDE, channels), jnp.float32),
            pltpu.VMEM((GROUPS * STRIDE, channels * width), jnp.float32),
            pltpu.VMEM((GROUPS * STRIDE, channels * width), jnp.float32),
            pltpu.VMEM(((rows + 2) * block, positions), jnp.bfloat16),
            pltpu.VMEM((count, each * width, positions), jnp.float32),
            pltpu.VMEM((count, each * width, positions), jnp.float32),
            pltpu.SemaphoreType.DMA((6,)),
            pltpu.SemaphoreType.DMA((count,)),
            pltpu.SemaphoreType.DMA((count,)),
        ],
        compiler_params=pltpu.CompilerParams(
            collective_id=0, has_side_effects=True, vmem_limit_bytes=60 * 1024 * 1024
        ),
        name="verify",
    )(
        round_owner,
        conv1_bias,
        queries.reshape(maps * rows * width, depth),
        db_maps.reshape(positions, depth),
        taps_first(conv1_weight),
        taps_first(conv2_weight),
    )
    return jnp.maximum(result + conv2_bias[0], 0.0).reshape(rounds, 1, each, width, positions)


def solution(mesh):
    placed = (
        P(("groups", "qrow"), None, None, None),
        P(("groups", "db", "rep"), None, None),
        P("groups"),
        P(),
        P(),
        P(),
        P(),
    )
    return jax.shard_map(
        functools.partial(on_device, mesh.shape["qrow"]),
        mesh=mesh,
        in_specs=placed,
        out_specs=P(None, ("groups", "db", "rep"), "qrow", None, None),
        check_vma=False,
    )
```
